32 devices in a mesh: det: 2 (over core), ord: 16 (over z, y, x).
Axes of the slice: x: 2, y: 2, z: 4, core: 2. Of those that a mesh axis runs over, the one named last changes fastest.
Arguments:
- wigner: bfloat16 [256, 2, 128, 2048], P('ord', None, None, 'det'), may hold values from -0.125 to 0.125
- alm: bfloat16 [256, 2, 2048], P('ord'), may hold values from -6 to 6
- beam: bfloat16 [64, 2, 2048], replicated, may hold values from -6 to 6
- crossing: int32 [16, 128], P('ord'), may hold values from 0 to 1023, as said below
- offsets: int32 [16, 4096], P('ord'), may hold values from 0 to 124
- fraction: float32 [16, 4096], P('ord'), may hold values from 0 to 1
- taps: float32 [33], replicated, may hold values from -1 to 1
Outputs:
- detector_signal: float32 [64, 65536], P('det', 'ord')
The draws below stay inside these ranges and needn't reach their ends.
Inputs may be any that keep to these rules, and one draw needn't show every extreme that they name: `crossing`: within one interval's 128 entries at most 16 lie in any one block of 64 consecutive ids; in every draw some block holds exactly 16 entries of every interval.
All inputs are finite; a program needn't handle non-finite values.
Results may differ from the reference program's by a relative error of at most 0.0057.
Values may be sent and summed in bfloat16 or wider, within the bound.
A program may use at most 192 MiB of HBM per device.

```python
import math
import jax
import jax.numpy as jnp
from jax import lax

L = 2048
M_DEV = 16
K = 2
LATS = 128
TILE = 128
CROSSINGS = 128
SAMPLES = 32
REACH = 16
TAPS = 33
M = 256
DETS = 64
INTERVALS = 16
TILES_DEV = 64
CAP = 16
TIME = 4096


def draw_crossing(key, part):
    entries = INTERVALS * CAP
    key_hot, key_score, key_order, key_local = jax.random.split(key, 4)
    hot_holder = jax.random.randint(key_hot, (), 0, INTERVALS)
    entry_ids = jnp.arange(entries, dtype=jnp.int32)
    holders = entry_ids // CAP
    scores = jax.random.randint(key_score, (INTERVALS, entries), 0, 1 << 20)
    first_row = jnp.arange(INTERVALS, dtype=jnp.int32)[:, None] == 0
    edge_entries = (entry_ids == 0) | (entry_ids == (INTERVALS - 1) * CAP)
    scores = jnp.where(first_row & edge_entries[None, :], -1, scores)
    scores = jnp.where(holders[None, :] == hot_holder, -2, scores)
    ranked = jnp.argsort(scores * entries + entry_ids[None, :], axis=1, stable=True)
    taken = ranked[:, :CROSSINGS]
    local_draws = jax.random.randint(key_local, (INTERVALS, entries), 0, TILES_DEV)
    local_draws = jnp.where(first_row & (entry_ids[None, :] == 0), 0, local_draws)
    local_draws = jnp.where(first_row & (entry_ids[None, :] == (INTERVALS - 1) * CAP), TILES_DEV - 1, local_draws)
    tile_ids = holders[None, :] * TILES_DEV + local_draws
    chosen = jnp.take_along_axis(tile_ids, taken, axis=1)
    order_scores = jax.random.randint(key_order, (INTERVALS, CROSSINGS), 0, 1 << 20) * CROSSINGS + jnp.arange(CROSSINGS, dtype=jnp.int32)[None, :]
    shuffle = jnp.argsort(order_scores, axis=1, stable=True)
    return jnp.take_along_axis(chosen, shuffle, axis=1).astype(jnp.int32)


def plant(values, key, low, largest):
    spot = [jax.random.randint(jax.random.fold_in(key, axis), (), 0, length) for axis, length in enumerate(values.shape)]
    longest = values.shape.index(max(values.shape))
    beside = spot[:longest] + [(spot[longest] + 1) % values.shape[longest]] + spot[longest + 1:]
    return values.at[tuple(spot)].set(low).at[tuple(beside)].set(largest)


def block_levels(rng, extent, shards, low, top_value):
    def one(dim, shards_of):
        draws = jax.random.uniform(jax.random.fold_in(jax.random.fold_in(rng, 6), dim), (shards_of,), jnp.float32, low / len(shards), top_value / len(shards))
        return jnp.repeat(jnp.exp(draws), extent[dim] // shards_of).reshape((-1,) + (1,) * (len(extent) - dim - 1))

    level = one(*shards[0])
    for cut in shards[1:]:
        level = level * one(*cut)
    return level


def bell_draw(rng, extent, width, most, shards=(), kind=jnp.bfloat16):
    values = jax.random.normal(rng, extent, jnp.float32) * width
    if len(shards) > 0:
        values = block_levels(rng, extent, shards, -0.22, 0.18) * values
    return jnp.clip(values, min=-most, max=most).astype(kind)


def setup_inputs(seed: int = 0) -> dict:
    streams_of = jax.random.split(jax.random.key(seed), 8)
    return {
        "wigner": bell_draw(streams_of[0], (M, K, LATS, L), L ** -0.5, 0.125, ((0, 16), (3, 2))),
        "alm": bell_draw(streams_of[1], (M, 2, L), 1.0, 6.0, ((0, 16),)),
        "beam": bell_draw(streams_of[2], (DETS, K, L), 1.0, 6.0),
        "crossing": draw_crossing(jax.random.fold_in(streams_of[7], 71), 0),
        "offsets": plant(jax.random.randint(streams_of[4], (INTERVALS, TIME), 0, TILE - 3), jax.random.fold_in(streams_of[4], 1), 0, (TILE - 3) - 1).astype(jnp.int32),
        "fraction": jnp.clip(1.0 * jax.random.uniform(streams_of[5], (INTERVALS, TIME), jnp.float32) ** block_levels(streams_of[5], (INTERVALS, TIME), ((0, 16),), -0.2, 0.2), 0.0, 1.0),
        "taps": bell_draw(streams_of[6], (TAPS,), TAPS ** -0.5, 1.0, (), jnp.float32),
    }


def lagrange_weights(position):
    shifted = position + 1.0
    minus_one = position - 1.0
    minus_two = position - 2.0
    return (-position * minus_one * minus_two / 6.0, shifted * minus_one * minus_two / 2.0, -shifted * position * minus_two / 2.0, shifted * position * minus_one / 6.0)

def reference(wigner, alm, beam, crossing, offsets, fraction, taps):
    orders = wigner.shape[0]
    groups = orders // M_DEV
    wigner_blocks = wigner.reshape(groups, M_DEV, K, LATS, L)
    alm_blocks = alm.reshape(groups, M_DEV, 2, L)
    beam_wide = beam.astype(jnp.float32)

    def spectra_block(operands):
        wigner_block, alm_block = operands
        coefficients = (beam_wide[:, None, :, None, :] * alm_block.astype(jnp.float32)[None, :, None, :, :]).astype(jnp.bfloat16)
        result = jnp.einsum('mkrl,jmkcl->jkrcm', wigner_block.astype(jnp.float32), coefficients.astype(jnp.float32), precision=lax.Precision.HIGHEST)
        return result.astype(jnp.bfloat16)
    spectra = lax.map(spectra_block, (wigner_blocks, alm_blocks))
    spectra = jnp.transpose(spectra, (2, 3, 1, 4, 0, 5)).reshape(K * LATS, DETS, 2, orders).astype(jnp.float32)
    longitudes = 2 * orders
    zero_column = jnp.zeros((K * LATS, DETS, 1), jnp.float32)
    real_part = jnp.concatenate([spectra[:, :, 0], zero_column], axis=2)
    imag_part = jnp.concatenate([spectra[:, :, 1], zero_column], axis=2)
    field = jnp.fft.irfft(real_part + 1j * imag_part, n=longitudes, axis=2) * (longitudes / math.sqrt(longitudes))
    cube = field.astype(jnp.bfloat16)
    blocks_per_item = longitudes // TILE

    def interval_samples(triple):
        wanted, offset_row, fraction_row = triple
        item = wanted // blocks_per_item
        start_column = wanted % blocks_per_item * TILE
        offset_rows = offset_row.reshape(CROSSINGS, SAMPLES)
        fraction_rows = fraction_row.reshape(CROSSINGS, SAMPLES)
        factors = lagrange_weights(fraction_rows)
        total = jnp.zeros((CROSSINGS, SAMPLES, DETS), jnp.float32)
        for place in range(4):
            columns = start_column[:, None] + offset_rows + place
            picked = cube[item[:, None], :, columns]
            total = total + factors[place][:, :, None] * picked.astype(jnp.float32)
        return jnp.transpose(total, (2, 0, 1)).reshape(DETS, CROSSINGS * SAMPLES).astype(jnp.bfloat16)
    samples = lax.map(interval_samples, (crossing, offsets, fraction))
    samples = jnp.transpose(samples, (1, 0, 2)).reshape(DETS, -1).astype(jnp.float32)
    padded = jnp.pad(samples, ((0, 0), (REACH, REACH)))
    span = samples.shape[1]
    signal = jnp.zeros_like(samples)
    for shift_index in range(TAPS):
        signal = signal + taps[shift_index] * padded[:, shift_index:shift_index + span]
    return signal
```

```python
import functools
import math

import jax
import jax.numpy as jnp
import numpy as np
from jax import lax
from jax.experimental import pallas as pl
from jax.experimental.pallas import tpu as pltpu
from jax.sharding import PartitionSpec as P

TILE = 128
CHUNKS = 4
INFO_ROWS = 40
MESH = pl.DeviceIdType.MESH


def split_parts(values):
    high = values.astype(jnp.bfloat16)
    return high, (values - high.astype(jnp.float32)).astype(jnp.bfloat16)


def fourier_tables(orders_total, per):
    longitudes = 2 * orders_total
    order = np.arange(orders_total, dtype=np.int64)
    phase = (order[:, None] * np.arange(longitudes)[None, :]) % longitudes
    angle = phase * (2.0 * math.pi / longitudes)
    weight = np.where(order == 0, 1.0, 2.0)[:, None] / math.sqrt(longitudes)
    parts = np.stack([weight * np.cos(angle), -weight * np.sin(angle)], axis=1)
    parts = parts.reshape(orders_total, 2, longitudes // TILE, TILE)
    table = np.zeros((orders_total, per, 2, longitudes // TILE, per, TILE), np.float32)
    for det in range(per):
        table[:, det, :, :, det, :] = parts
    table = table.reshape(orders_total * per * 2, longitudes * per)
    high = table.astype(jnp.bfloat16)
    low = (table - high.astype(np.float32)).astype(jnp.bfloat16)
    return np.stack([high, low])


def kernel(
    count, per, intervals, tiles_per_item,
    wigner_hbm, beam_ref, alm_ref, table_hbm, info_ref, taps_ref,
    out_ref,
    wigner, table, partial_own, partial_out, partial_in, spectra_out, spectra_in,
    info, picks, shifts, weights, band, cube, series, signal_out,
    wigner_sem, table_sem, info_send, info_recv, share_send, share_recv,
    pair_send, pair_recv, spec_send, spec_recv, out_send, out_recv,
):
    det = lax.axis_index("det")
    me = lax.axis_index("ord")
    partner = 1 - det
    orders = wigner.shape[0]
    chunk_orders = orders // CHUNKS
    blocks = shifts.shape[2]
    groups = tiles_per_item

    def wigner_copy(chunk):
        part = pl.ds(chunk * chunk_orders, chunk_orders)
        return pltpu.make_async_copy(wigner_hbm.at[part], wigner.at[part], wigner_sem.at[chunk])

    for chunk in range(CHUNKS):
        wigner_copy(chunk).start()
    table_copy = pltpu.make_async_copy(table_hbm, table, table_sem)
    table_copy.start()

    barrier = pltpu.get_barrier_semaphore()

    def greet(step, carry):
        peer = lax.rem(me + step, count)
        pl.semaphore_signal(barrier, inc=1, device_id=(det, peer), device_id_type=MESH)
        return carry

    lax.fori_loop(1, count, greet, 0)
    pl.semaphore_signal(barrier, inc=1, device_id=(partner, me), device_id_type=MESH)
    pl.semaphore_wait(barrier, count)

    info[det, me] = info_ref[...]

    def info_copy(target, source):
        return pltpu.make_async_remote_copy(
            src_ref=info_ref,
            dst_ref=info.at[det, source],
            send_sem=info_send.at[target],
            recv_sem=info_recv.at[source],
            device_id=(det, target),
            device_id_type=MESH,
        )

    def info_start(step, carry):
        info_copy(lax.rem(me + step, count), me).start()
        return carry

    lax.fori_loop(1, count, info_start, 0)

    rows = per * 2
    own_rows = count * rows

    def product(order, beam_order):
        alm_rows = alm_ref[order]
        beam_rows = beam_ref[beam_order]
        depth = beam_rows.shape[1]
        sky = beam_rows.reshape(-1, alm_rows.shape[0], depth) * alm_rows[None]
        return lax.dot_general(
            sky.reshape(-1, depth),
            wigner[order, beam_order],
            (((1,), (1,)), ((), ())),
            preferred_element_type=jnp.float32,
        )

    def multiply(chunk):
        wigner_copy(chunk).wait()

        def pair(step, carry):
            first = chunk * chunk_orders + 2 * step
            place = pl.ds(pl.multiple_of(step * 2 * rows, 2 * rows), 2 * rows)
            for beam_order in range(wigner.shape[1]):
                lanes = pl.ds(beam_order * wigner.shape[2], wigner.shape[2])
                one = product(first, beam_order)
                two = product(first + 1, beam_order)
                for target, low in ((partial_own, 0), (partial_out, own_rows)):
                    target[chunk, :, place, lanes] = jnp.concatenate(
                        [
                            one[low : low + own_rows].reshape(count, rows, -1),
                            two[low : low + own_rows].reshape(count, rows, -1),
                        ],
                        axis=1,
                    )
            return carry

        lax.fori_loop(0, chunk_orders // 2, pair, 0)

    def pair_copy(chunk):
        return pltpu.make_async_remote_copy(
            src_ref=partial_out.at[chunk],
            dst_ref=partial_in.at[chunk],
            send_sem=pair_send.at[chunk],
            recv_sem=pair_recv.at[chunk],
            device_id=(partner, me),
            device_id_type=MESH,
        )

    def spec_copy(chunk, target, source):
        return pltpu.make_async_remote_copy(
            src_ref=spectra_out.at[chunk, target],
            dst_ref=spectra_in.at[source, chunk],
            send_sem=spec_send.at[chunk, target],
            recv_sem=spec_recv.at[chunk, source],
            device_id=(det, target),
            device_id_type=MESH,
        )

    def spread(chunk):
        pair_copy(chunk).wait_recv()
        total = (partial_own[chunk] + partial_in[chunk]).astype(jnp.bfloat16)
        spectra_out[chunk] = total

        def start(step, carry):
            spec_copy(chunk, lax.rem(me + step, count), me).start()
            return carry

        lax.fori_loop(1, count, start, 0)
        spectra_in[me, chunk] = spectra_out[chunk, me]

    for chunk in range(CHUNKS):
        multiply(chunk)
        pair_copy(chunk).start()
        if chunk > 0:
            spread(chunk - 1)
    spread(CHUNKS - 1)

    def info_wait(step, carry):
        source = lax.rem(me + count - step, count)
        info_copy(source, source).wait_recv()
        return carry

    lax.fori_loop(1, count, info_wait, 0)
    share_copy = pltpu.make_async_remote_copy(
        src_ref=info.at[det],
        dst_ref=info.at[det],
        send_sem=share_send,
        recv_sem=share_recv,
        device_id=(partner, me),
        device_id_type=MESH,
    )
    share_copy.start()

    shape = (3 * TILE, TILE)
    lag = (
        lax.broadcasted_iota(jnp.int32, shape, 0) - lax.broadcasted_iota(jnp.int32, shape, 1)
    )
    reach = taps_ref.shape[0] // 2

    def add_tap(place, total):
        return jnp.where(lag == place + (TILE - reach), taps_ref[place], total)

    band_values = lax.fori_loop(0, taps_ref.shape[0], add_tap, jnp.zeros(shape, jnp.float32))
    band_high, band_low = split_parts(band_values)
    band[0] = band_high
    band[1] = band_low

    pltpu.make_async_remote_copy(
        src_ref=info.at[partner],
        dst_ref=info.at[partner],
        send_sem=share_send,
        recv_sem=share_recv,
        device_id=(partner, me),
        device_id_type=MESH,
    ).wait_recv()

    lane = lax.broadcasted_iota(jnp.int32, (blocks, TILE), 1)
    each = TILE // groups
    group = lane // each
    items = cube.shape[0] // groups
    half_rows = blocks // 2

    def prepare(n, carry):
        wanted = info[0, n, 2 * half_rows : 2 * half_rows + 1, :]
        ids = jnp.broadcast_to(wanted, (TILE, TILE)).T
        for part in range(cube.shape[0] // TILE):
            places = lax.broadcasted_iota(jnp.int32, (TILE, TILE), 1) + part * TILE
            picks[n, :, part * TILE : (part + 1) * TILE] = jnp.where(
                ids == places.astype(jnp.float32), 1.0, 0.0
            ).astype(jnp.bfloat16)
        offset = jnp.concatenate([info[0, n, :half_rows], info[1, n, :half_rows]], axis=0)
        fraction = jnp.concatenate(
            [info[0, n, half_rows : 2 * half_rows], info[1, n, half_rows : 2 * half_rows]],
            axis=0,
        )
        for b in range(groups):
            spot = b * each + lane % each
            start = jnp.take_along_axis(offset, spot, axis=1, mode="promise_in_bounds")
            f = jnp.take_along_axis(fraction, spot, axis=1, mode="promise_in_bounds")
            shifts[n, b] = start.astype(jnp.int32) + group
            weights[n, b] = (
                jnp.where(group == 0, -1.0 / 6.0, f + 1.0)
                * jnp.where(group == 1, 0.5, f)
                * jnp.where(group == 2, -0.5, f - 1.0)
                * jnp.where(group == 3, 1.0 / 6.0, f - 2.0)
            )
        return carry

    lax.fori_loop(0, intervals, prepare, 0)

    table_copy.wait()
    for chunk in range(CHUNKS):
        def spec_wait(step, carry, chunk=chunk):
            source = lax.rem(me + count - step, count)
            spec_copy(chunk, source, source).wait_recv()
            return carry

        lax.fori_loop(1, count, spec_wait, 0)

    spectra = spectra_in[...].reshape(-1, items)
    for b in range(groups):
        columns = pl.ds(b * per * TILE, per * TILE)
        field = lax.dot_general(
            spectra,
            table[0, :, columns],
            (((0,), (0,)), ((), ())),
            preferred_element_type=jnp.float32,
        ) + lax.dot_general(
            spectra,
            table[1, :, columns],
            (((0,), (0,)), ((), ())),
            preferred_element_type=jnp.float32,
        )
        cube[b * items : (b + 1) * items] = field.astype(jnp.bfloat16)

    margin = 8
    for d in range(per):
        series[d, :margin] = jnp.zeros((margin, TILE), jnp.float32)
        series[d, margin + intervals * blocks :] = jnp.zeros((margin, TILE), jnp.float32)

    def sample(n, carry):
        tiles = jnp.dot(picks[n], cube[...], preferred_element_type=jnp.float32)
        for d in range(per):
            terms = [
                jnp.take_along_axis(
                    tiles[b * blocks : (b + 1) * blocks, d * TILE : (d + 1) * TILE],
                    shifts[n, b],
                    axis=1,
                    mode="promise_in_bounds",
                )
                * weights[n, b]
                for b in range(groups)
            ]
            total = jnp.zeros((blocks, TILE), jnp.float32)
            for k in range(groups):
                moved = terms[(groups - 1 - k) % groups]
                for t in range(groups - 1):
                    moved = jnp.where(group == t, terms[(t - k) % groups], moved)
                if k:
                    moved = pltpu.roll(moved, TILE - k * each, 1)
                total = total + moved
            place = pl.ds(pl.multiple_of(margin + n * blocks, 8), blocks)
            series[d, place] = total.astype(jnp.bfloat16).astype(jnp.float32)
        return carry

    lax.fori_loop(0, intervals, sample, 0)

    def out_copy(target, source):
        return pltpu.make_async_remote_copy(
            src_ref=signal_out.at[target],
            dst_ref=out_ref.at[source],
            send_sem=out_send.at[target],
            recv_sem=out_recv.at[source],
            device_id=(det, target),
            device_id_type=MESH,
        )

    def smooth(n):
        windows = []
        for d in range(per):
            near = series[d, pl.ds(pl.multiple_of(n * blocks, 8), blocks + 2 * margin)]
            windows.append(
                jnp.concatenate(
                    [near[margin + s : margin + s + blocks] for s in (-1, 0, 1)], axis=1
                )
            )
        window = jnp.concatenate(windows, axis=0).astype(jnp.bfloat16)
        smoothed = jnp.dot(window, band[0], preferred_element_type=jnp.float32) + jnp.dot(
            window, band[1], preferred_element_type=jnp.float32
        )
        return smoothed.astype(jnp.bfloat16).reshape(per, blocks, TILE)

    def finish(step, carry):
        target = lax.rem(me + step, count)
        signal_out[target] = smooth(target)
        out_copy(target, me).start()
        return carry

    lax.fori_loop(1, count, finish, 0)
    out_ref[me] = smooth(me)

    def drain(step, carry):
        target = lax.rem(me + step, count)
        info_copy(target, me).wait_send()
        for chunk in range(CHUNKS):
            spec_copy(chunk, target, me).wait_send()
        out_copy(target, me).wait_send()
        source = lax.rem(me + count - step, count)
        out_copy(source, source).wait_recv()
        return carry

    lax.fori_loop(1, count, drain, 0)
    for chunk in range(CHUNKS):
        pair_copy(chunk).wait_send()
    share_copy.wait_send()


def local_fused(wigner, alm, beam, crossing, offsets, fraction, taps):
    det_count = lax.axis_size("det")
    det = lax.axis_index("det")
    count = lax.axis_size("ord")
    orders, beams, lats, depth = wigner.shape
    dets = beam.shape[0]
    per = dets // det_count // count
    orders_total = orders * count
    longitudes = 2 * orders_total
    groups = longitudes // TILE
    items = beams * lats
    tiles = items * groups
    intervals = count
    blocks = offsets.shape[1] // TILE
    chunk_rows = orders // CHUNKS * per * 2

    beam_half = lax.dynamic_slice_in_dim(beam, det * depth, depth, 2)
    beam_pair = beam_half.reshape(det_count, -1, beams, depth)
    beam_pair = jnp.where(det == 0, beam_pair, beam_pair[::-1]).reshape(dets, beams, depth)
    beam_rows = jnp.repeat(jnp.transpose(beam_pair, (1, 0, 2)), 2, axis=1)
    alm_half = lax.dynamic_slice_in_dim(alm, det * depth, depth, 2)
    alm_rows = jnp.tile(alm_half, (1, 8, 1))

    wanted = (crossing[0] % groups) * items + crossing[0] // groups
    wanted = wanted.reshape(blocks, -1).T.reshape(1, TILE).astype(jnp.float32)
    half = blocks // 2
    info = jnp.concatenate(
        [
            lax.dynamic_slice_in_dim(
                offsets.reshape(blocks, TILE), det * half, half, 0
            ).astype(jnp.float32),
            lax.dynamic_slice_in_dim(fraction.reshape(blocks, TILE), det * half, half, 0),
            jnp.broadcast_to(wanted, (INFO_ROWS - 2 * half, TILE)),
        ],
        axis=0,
    )
    table = jnp.asarray(fourier_tables(orders_total, per))

    f32, bf16 = jnp.float32, jnp.bfloat16
    dma = pltpu.SemaphoreType.DMA
    vmem = pl.BlockSpec(memory_space=pltpu.VMEM)
    anywhere = pl.BlockSpec(memory_space=pl.ANY)
    partial = pltpu.VMEM((CHUNKS, count, chunk_rows, items), f32)
    outgoing = pltpu.VMEM((CHUNKS, count, chunk_rows, items), bf16)
    arriving = pltpu.VMEM((count, CHUNKS, chunk_rows, items), bf16)
    result = pl.pallas_call(
        functools.partial(kernel, count, per, intervals, groups),
        out_shape=jax.ShapeDtypeStruct((count, per, blocks, TILE), bf16),
        in_specs=[
            anywhere, vmem, vmem, anywhere, vmem,
            pl.BlockSpec(memory_space=pltpu.SMEM),
        ],
        out_specs=vmem,
        scratch_shapes=[
            pltpu.VMEM(wigner.shape, bf16),
            pltpu.VMEM(table.shape, bf16),
            partial, partial, partial, outgoing, arriving,
            pltpu.VMEM((2, count, INFO_ROWS, TILE), f32),
            pltpu.VMEM((intervals, TILE, tiles), bf16),
            pltpu.VMEM((intervals, groups, blocks, TILE), jnp.int32),
            pltpu.VMEM((intervals, groups, blocks, TILE), f32),
            pltpu.VMEM((2, 3 * TILE, TILE), bf16),
            pltpu.VMEM((tiles, per * TILE), bf16),
            pltpu.VMEM((per, intervals * blocks + 16, TILE), f32),
            pltpu.VMEM((count, per, blocks, TILE), bf16),
            dma((CHUNKS,)), dma, dma((count,)), dma((count,)), dma, dma,
            dma((CHUNKS,)), dma((CHUNKS,)), dma((CHUNKS, count)), dma((CHUNKS, count)),
            dma((count,)), dma((count,)),
        ],
        compiler_params=pltpu.CompilerParams(
            collective_id=0, has_side_effects=True, vmem_limit_bytes=56 * 2**20
        ),
    )(wigner, beam_rows, alm_rows, table, info, taps)
    return result.astype(f32).reshape(count * per, blocks * TILE)


def with_halo(cells, sides, width):
    for axis, dim in sides:
        count = lax.axis_size(axis)
        ends = count - 1
        head = lax.slice_in_dim(cells, 0, width, axis=dim)
        tail = lax.slice_in_dim(cells, cells.shape[dim] - width, cells.shape[dim], axis=dim)
        cells = jnp.concatenate(
            [
                lax.ppermute(tail, axis, [(i, (i + 1) % count) for i in range(ends)]),
                cells,
                lax.ppermute(head, axis, [((i + 1) % count, i) for i in range(ends)]),
            ],
            axis=dim,
        )
    return cells


def lagrange_weights(position):
    shifted = position + 1.0
    minus_one = position - 1.0
    minus_two = position - 2.0
    return (
        -position * minus_one * minus_two / 6.0,
        shifted * minus_one * minus_two / 2.0,
        -shifted * position * minus_two / 2.0,
        shifted * position * minus_one / 6.0,
    )


def stencil_matrix(offset_part, fraction_part, width):
    columns = jnp.arange(width, dtype=jnp.int32)
    distance = columns[:, None] - offset_part[..., None, :]
    factors = lagrange_weights(fraction_part[..., None, :])
    matrix = jnp.zeros(distance.shape, jnp.float32)
    for place in range(4):
        matrix = matrix + jnp.where(distance == place, factors[place], 0.0)
    return matrix


def sky_beam(alm_part, beam_part):
    product = (
        beam_part.astype(jnp.float32)[:, None, :, None, :]
        * alm_part.astype(jnp.float32)[None, :, None, :, :]
    )
    return product.astype(jnp.bfloat16)


def local(wigner, alm, beam, crossing, offsets, fraction, taps):
    det_count = lax.axis_size("det")
    det_index = lax.axis_index("det")
    ord_count = lax.axis_size("ord")
    orders_local = wigner.shape[0]
    half_width = wigner.shape[3]
    det_local = beam.shape[0] // det_count
    alm_half = lax.dynamic_slice_in_dim(alm, det_index * half_width, half_width, 2)
    beam_half = lax.dynamic_slice_in_dim(beam, det_index * half_width, half_width, 2)
    spectra = lax.psum_scatter(
        jnp.einsum(
            "mkrl,jmkcl->jkrcm",
            wigner,
            sky_beam(alm_half, beam_half),
            preferred_element_type=jnp.float32,
        ),
        "det",
        scatter_dimension=0,
        tiled=True,
    )
    items_all = wigner.shape[1] * wigner.shape[2]
    outgoing = spectra.astype(jnp.bfloat16).reshape(det_local, items_all, 2 * orders_local)
    arrived = lax.all_to_all(outgoing, "ord", split_axis=1, concat_axis=2, tiled=True)
    items_local = items_all // ord_count
    spectrum = arrived.reshape(det_local, items_local, ord_count, 2, orders_local).astype(
        jnp.float32
    )
    orders_total = ord_count * orders_local
    longitudes = 2 * orders_total
    block = math.gcd(512, longitudes)
    order_ids = (
        jnp.arange(ord_count, dtype=jnp.int32)[:, None] * orders_local
        + jnp.arange(orders_local, dtype=jnp.int32)[None, :]
    )
    weight_row = (jnp.where(order_ids == 0, 1.0, 2.0) / math.sqrt(longitudes))[:, :, None]
    step_angle = 2.0 * math.pi / longitudes
    base_phase = (
        order_ids[:, :, None] * jnp.arange(block, dtype=jnp.int32)[None, None, :] % longitudes
    )
    base_angle = base_phase.astype(jnp.float32) * step_angle
    base_cos = jnp.cos(base_angle)
    base_sin = jnp.sin(base_angle)
    pieces = []
    for first in range(0, longitudes, block):
        shift_angle = (order_ids * first % longitudes).astype(jnp.float32)[:, :, None] * step_angle
        shift_cos = jnp.cos(shift_angle)
        shift_sin = jnp.sin(shift_angle)
        cos_block = base_cos * shift_cos - base_sin * shift_sin
        sin_block = base_sin * shift_cos + base_cos * shift_sin
        table = jnp.stack([weight_row * cos_block, -weight_row * sin_block], axis=1)
        pieces.append(
            jnp.einsum("jincs,ncsp->ijp", spectrum, table, precision=lax.Precision.HIGHEST)
        )
    cube = jnp.concatenate(pieces, axis=2).astype(jnp.bfloat16)
    tile_width = TILE
    blocks_per_item = longitudes // tile_width
    tiles = cube.reshape(items_local, det_local, blocks_per_item, tile_width).transpose(0, 2, 1, 3)
    tiles = tiles.reshape(items_local * blocks_per_item, det_local, tile_width)
    tiles_local = tiles.shape[0]
    wanted = crossing[0]
    crossings = wanted.shape[0]
    capacity = max(2, 2 * crossings // ord_count)
    holder = wanted // tiles_local
    local_ids = wanted % tiles_local
    order_index = jnp.arange(crossings, dtype=jnp.int32)
    earlier = (holder[:, None] == holder[None, :]) & (order_index[None, :] < order_index[:, None])
    slot_ids = jnp.sum(earlier.astype(jnp.int32), axis=1)
    flat_slot = holder * capacity + slot_ids
    chosen = flat_slot[:, None] == jnp.arange(ord_count * capacity, dtype=jnp.int32)[None, :]
    requests = (jnp.sum(jnp.where(chosen, local_ids[:, None] + 1, 0), axis=0) - 1).reshape(
        ord_count, capacity
    )
    offset_rows = offsets[0].reshape(crossings, -1)
    fraction_rows = fraction[0].reshape(crossings, -1)
    samples_each = offset_rows.shape[1]
    slot_crossing = jnp.sum(jnp.where(chosen, order_index[:, None], 0), axis=0)
    occupied = jnp.any(chosen, axis=0)
    slot_offsets = jnp.where(occupied[:, None], offset_rows[slot_crossing], 0)
    slot_offsets = slot_offsets.reshape(ord_count, capacity, samples_each)
    slot_fractions = jnp.where(occupied[:, None], fraction_rows[slot_crossing], 0.0)
    slot_fractions = slot_fractions.reshape(ord_count, capacity, samples_each)
    asked = lax.all_to_all(requests, "ord", split_axis=0, concat_axis=0, tiled=True)
    asked_offsets = lax.all_to_all(slot_offsets, "ord", split_axis=0, concat_axis=0, tiled=True)
    asked_fractions = lax.all_to_all(slot_fractions, "ord", split_axis=0, concat_axis=0, tiled=True)
    stencil = stencil_matrix(asked_offsets, asked_fractions, tile_width)
    present = asked >= 0
    picked = tiles[jnp.maximum(asked, 0)]
    result = jnp.einsum(
        "rnjo,rnos->rnjs",
        jnp.where(present[..., None, None], picked, jnp.zeros((), jnp.bfloat16)).astype(
            jnp.float32
        ),
        stencil,
        precision=lax.Precision.HIGHEST,
    )
    received = lax.all_to_all(
        result.astype(jnp.bfloat16), "ord", split_axis=0, concat_axis=0, tiled=True
    )
    samples = jnp.transpose(received[holder, slot_ids], (1, 0, 2)).reshape(det_local, -1)
    reach = taps.shape[0] // 2
    extended = with_halo(samples, (("ord", 1),), reach)
    total_time = samples.shape[1]
    padded = jnp.concatenate(
        [extended, jnp.zeros((det_local, 128 - 2 * reach), jnp.bfloat16)], axis=1
    )
    windows = jnp.concatenate(
        [
            padded[:, :total_time].reshape(det_local, -1, 128),
            padded[:, 128 : total_time + 128].reshape(det_local, -1, 128),
        ],
        axis=2,
    )
    lag_index = (
        jnp.arange(256, dtype=jnp.int32)[:, None] - jnp.arange(128, dtype=jnp.int32)[None, :]
    )
    inside = (lag_index >= 0) & (lag_index < taps.shape[0])
    banded = jnp.where(inside, taps[jnp.clip(lag_index, 0, taps.shape[0] - 1)], 0.0)
    smoothed = jnp.einsum(
        "jbu,uo->jbo", windows.astype(jnp.float32), banded, precision=lax.Precision.HIGHEST
    )
    return smoothed.reshape(det_local, total_time)


def splits_detectors(mesh, wigner, beam, offsets):
    count = mesh.shape["ord"]
    return (
        mesh.shape["det"] == 2
        and beam.shape[0] == 4 * count
        and wigner.shape[0] == 4 * CHUNKS * count
        and 2 * wigner.shape[0] == 4 * TILE
        and wigner.shape[1:3] == (2, TILE)
        and offsets.shape == (count, 32 * TILE)
    )


def solution(mesh):
    def run(wigner, alm, beam, crossing, offsets, fraction, taps):
        fused = splits_detectors(mesh, wigner, beam, offsets)
        return jax.shard_map(
            local_fused if fused else local,
            mesh=mesh,
            in_specs=(
                P("ord", None, None, "det"),
                P("ord", None, None),
                P(),
                P("ord", None),
                P("ord", None),
                P("ord", None),
                P(),
            ),
            out_specs=P("det", "ord"),
            check_vma=False,
        )(wigner, alm, beam, crossing, offsets, fraction, taps)

    return run
```

```python
import functools
import math

import jax
import jax.numpy as jnp
import numpy as np
from jax import lax
from jax.experimental import pallas as pl
from jax.experimental.pallas import tpu as pltpu
from jax.sharding import PartitionSpec as P

TILE = 128
CHUNKS = 4
BATCH = 4
INFO_ROWS = 40
MESH = pl.DeviceIdType.MESH


def split_parts(values):
    high = values.astype(jnp.bfloat16)
    return high, (values - high.astype(jnp.float32)).astype(jnp.bfloat16)


def fourier_tables(orders_total, per):
    longitudes = 2 * orders_total
    order = np.arange(orders_total, dtype=np.int64)
    phase = (order[:, None] * np.arange(longitudes)[None, :]) % longitudes
    angle = phase * (2.0 * math.pi / longitudes)
    weight = np.where(order == 0, 1.0, 2.0)[:, None] / math.sqrt(longitudes)
    parts = np.stack([weight * np.cos(angle), -weight * np.sin(angle)], axis=1)
    parts = parts.reshape(orders_total, 2, longitudes // TILE, TILE)
    table = np.zeros((orders_total, per, 2, longitudes // TILE, per, TILE), np.float32)
    for det in range(per):
        table[:, det, :, :, det, :] = parts
    table = table.reshape(orders_total * per * 2, longitudes * per)
    high = table.astype(jnp.bfloat16)
    low = (table - high.astype(np.float32)).astype(jnp.bfloat16)
    return np.stack([high, low])


def kernel(
    count, per, intervals, tiles_per_item,
    wigner_hbm, beam_hbm, alm_hbm, table_hbm, crossing_ref, offsets_ref, fraction_ref, taps_ref,
    out_ref,
    beam_in, alm_in, beam_ref, alm_ref,
    wigner, table, partial_own, partial_out, partial_in, spectra_out, spectra_in,
    info_ref, info, picks, shifts, weights, band, field, cube, tiles, series,
    signal_out, signal_in,
    small_sem, wigner_sem, table_sem, info_send, info_recv, share_send, share_recv,
    pair_send, pair_recv, spec_send, spec_recv, out_send, out_recv,
):
    det = lax.axis_index("det")
    me = lax.axis_index("ord")
    partner = 1 - det
    orders = wigner.shape[0]
    chunk_orders = orders // CHUNKS
    blocks = shifts.shape[2]
    groups = tiles_per_item

    def wigner_copy(chunk):
        part = pl.ds(chunk * chunk_orders, chunk_orders)
        return pltpu.make_async_copy(wigner_hbm.at[part], wigner.at[part], wigner_sem.at[chunk])

    depth = beam_in.shape[1]
    near_depth = pl.ds(pl.multiple_of(det * depth, TILE), depth)
    beam_copy = pltpu.make_async_copy(beam_hbm.at[:, near_depth], beam_in, small_sem.at[0])
    alm_copy = pltpu.make_async_copy(alm_hbm.at[:, near_depth], alm_in, small_sem.at[1])
    beam_copy.start()
    alm_copy.start()
    for chunk in range(CHUNKS):
        wigner_copy(chunk).start()
    table_copy = pltpu.make_async_copy(table_hbm, table, table_sem)
    table_copy.start()

    barrier = pltpu.get_barrier_semaphore()

    def greet(step, carry):
        peer = lax.rem(me + step, count)
        pl.semaphore_signal(barrier, inc=1, device_id=(det, peer), device_id_type=MESH)
        return carry

    lax.fori_loop(1, count, greet, 0)
    pl.semaphore_signal(barrier, inc=1, device_id=(partner, me), device_id_type=MESH)

    def select_rows(source, wanted_column):
        chosen = jnp.where(
            wanted_column == lax.broadcasted_iota(jnp.int32, wanted_column.shape, 1), 1.0, 0.0
        ).astype(jnp.bfloat16)
        return jnp.dot(chosen, source, preferred_element_type=jnp.float32).astype(jnp.bfloat16)

    beams = wigner.shape[1]
    beam_copy.wait()
    beam_rows_all = beam_ref.shape[1]
    row = lax.broadcasted_iota(jnp.int32, (beam_rows_all, beam_in.shape[0]), 0)
    half_rows = beam_rows_all // 2
    side = lax.rem(row // half_rows + det, 2)
    beam_column = (side * (half_rows // 2) + row % half_rows // 2) * beams
    for beam_order in range(beams):
        beam_ref[beam_order] = select_rows(beam_in[...], beam_column + beam_order)
    alm_copy.wait()
    repeat = alm_ref.shape[1]
    row = lax.broadcasted_iota(jnp.int32, (orders * repeat, alm_in.shape[0]), 0)
    alm_ref[...] = select_rows(alm_in[...], row // repeat * 2 + row % 2).reshape(
        alm_ref.shape
    )

    half_blocks = blocks // 2
    near_blocks = pl.ds(pl.multiple_of(det * half_blocks, 8), half_blocks)
    info_ref[:half_blocks] = offsets_ref[near_blocks].astype(jnp.float32)
    info_ref[half_blocks : 2 * half_blocks] = fraction_ref[near_blocks]
    ids = jnp.broadcast_to(crossing_ref[...], (8, TILE))
    ids = ids % groups * (cube.shape[0] // groups) + ids // groups
    lanes_row = lax.broadcasted_iota(jnp.int32, (8, TILE), 1)
    info_ref[2 * half_blocks :] = jnp.take_along_axis(
        ids.astype(jnp.float32),
        lanes_row % blocks * groups + lanes_row // blocks,
        axis=1,
        mode="promise_in_bounds",
    )

    def info_copy(target, source):
        return pltpu.make_async_remote_copy(
            src_ref=info_ref,
            dst_ref=info.at[det, source],
            send_sem=info_send.at[target],
            recv_sem=info_recv.at[source],
            device_id=(det, target),
            device_id_type=MESH,
        )

    def info_start(step, carry):
        info_copy(lax.rem(me + step, count), me).start()
        return carry

    rows = per * 2
    own_rows = count * rows

    def product(order, beam_order):
        alm_rows = alm_ref[order]
        beam_rows = beam_ref[beam_order]
        sky = beam_rows.reshape(-1, alm_rows.shape[0], depth) * alm_rows[None]
        return lax.dot_general(
            sky.reshape(-1, depth),
            wigner[order, beam_order],
            (((1,), (1,)), ((), ())),
            preferred_element_type=jnp.float32,
        )

    def multiply(chunk):
        wigner_copy(chunk).wait()

        def pair(step, carry):
            first = chunk * chunk_orders + 2 * step
            place = pl.ds(pl.multiple_of(step * 2 * rows, 2 * rows), 2 * rows)
            for beam_order in range(wigner.shape[1]):
                lanes = pl.ds(beam_order * wigner.shape[2], wigner.shape[2])
                one = product(first, beam_order)
                two = product(first + 1, beam_order)
                for target, low in ((partial_own, 0), (partial_out, own_rows)):
                    target[chunk, :, place, lanes] = jnp.concatenate(
                        [
                            one[low : low + own_rows].reshape(count, rows, -1),
                            two[low : low + own_rows].reshape(count, rows, -1),
                        ],
                        axis=1,
                    )
            return carry

        lax.fori_loop(0, chunk_orders // 2, pair, 0)

    def pair_copy(chunk):
        return pltpu.make_async_remote_copy(
            src_ref=partial_out.at[chunk],
            dst_ref=partial_in.at[chunk],
            send_sem=pair_send.at[chunk],
            recv_sem=pair_recv.at[chunk],
            device_id=(partner, me),
            device_id_type=MESH,
        )

    def spec_copy(chunk, target, source):
        return pltpu.make_async_remote_copy(
            src_ref=spectra_out.at[chunk, target],
            dst_ref=spectra_in.at[source, chunk],
            send_sem=spec_send.at[chunk, target],
            recv_sem=spec_recv.at[chunk, source],
            device_id=(det, target),
            device_id_type=MESH,
        )

    def spread(chunk):
        pair_copy(chunk).wait_recv()
        total = (partial_own[chunk] + partial_in[chunk]).astype(jnp.bfloat16)
        spectra_out[chunk] = total

        def start(step, carry):
            spec_copy(chunk, lax.rem(me + step, count), me).start()
            return carry

        lax.fori_loop(1, count, start, 0)
        spectra_in[me, chunk] = spectra_out[chunk, me]

    for chunk in range(CHUNKS):
        multiply(chunk)
        if chunk == 0:
            pl.semaphore_wait(barrier, count)
            info[det, me] = info_ref[...]
            lax.fori_loop(1, count, info_start, 0)
        pair_copy(chunk).start()
        if chunk > 0:
            spread(chunk - 1)
    spread(CHUNKS - 1)

    def info_wait(step, carry):
        source = lax.rem(me + count - step, count)
        info_copy(source, source).wait_recv()
        return carry

    lax.fori_loop(1, count, info_wait, 0)
    share_copy = pltpu.make_async_remote_copy(
        src_ref=info.at[det],
        dst_ref=info.at[det],
        send_sem=share_send,
        recv_sem=share_recv,
        device_id=(partner, me),
        device_id_type=MESH,
    )
    share_copy.start()

    shape = (3 * TILE, TILE)
    lag = (
        lax.broadcasted_iota(jnp.int32, shape, 0) - lax.broadcasted_iota(jnp.int32, shape, 1)
    )
    reach = taps_ref.shape[0] // 2

    def add_tap(place, total):
        return jnp.where(lag == place + (TILE - reach), taps_ref[place], total)

    band_values = lax.fori_loop(0, taps_ref.shape[0], add_tap, jnp.zeros(shape, jnp.float32))
    band_high, band_low = split_parts(band_values)
    band[0] = band_high
    band[1] = band_low

    pltpu.make_async_remote_copy(
        src_ref=info.at[partner],
        dst_ref=info.at[partner],
        send_sem=share_send,
        recv_sem=share_recv,
        device_id=(partner, me),
        device_id_type=MESH,
    ).wait_recv()

    lane = lax.broadcasted_iota(jnp.int32, (blocks, TILE), 1)
    each = TILE // groups
    group = lane // each
    items = cube.shape[0] // groups
    half_rows = blocks // 2

    def prepare(n, carry):
        wanted = info[0, n, 2 * half_rows : 2 * half_rows + 1, :]
        ids = jnp.broadcast_to(wanted, (TILE, TILE)).T
        for part in range(cube.shape[0] // TILE):
            places = lax.broadcasted_iota(jnp.int32, (TILE, TILE), 1) + part * TILE
            picks[n, :, part * TILE : (part + 1) * TILE] = jnp.where(
                ids == places.astype(jnp.float32), 1.0, 0.0
            ).astype(jnp.bfloat16)
        offset = jnp.concatenate([info[0, n, :half_rows], info[1, n, :half_rows]], axis=0)
        fraction = jnp.concatenate(
            [info[0, n, half_rows : 2 * half_rows], info[1, n, half_rows : 2 * half_rows]],
            axis=0,
        )
        for b in range(groups):
            spot = b * each + lane % each
            start = jnp.take_along_axis(offset, spot, axis=1, mode="promise_in_bounds")
            f = jnp.take_along_axis(fraction, spot, axis=1, mode="promise_in_bounds")
            shifts[n, b] = start.astype(jnp.int32) + group
            weights[n, b] = (
                jnp.where(group == 0, -1.0 / 6.0, f + 1.0)
                * jnp.where(group == 1, 0.5, f)
                * jnp.where(group == 2, -0.5, f - 1.0)
                * jnp.where(group == 3, 1.0 / 6.0, f - 2.0)
            )
        return carry

    lax.fori_loop(0, intervals, prepare, 0)

    table_copy.wait()
    chunk_rows = spectra_in.shape[2]
    for chunk in range(CHUNKS):
        def spec_wait(step, carry, chunk=chunk):
            source = lax.rem(me + count - step, count)
            spec_copy(chunk, source, source).wait_recv()
            return carry

        lax.fori_loop(1, count, spec_wait, 0)
        spectra = spectra_in[:, chunk].reshape(count * chunk_rows, items)
        for b in range(groups):
            columns = pl.ds(b * per * TILE, per * TILE)
            total = sum(
                lax.dot_general(
                    spectra,
                    table[part, chunk, :, columns],
                    (((0,), (0,)), ((), ())),
                    preferred_element_type=jnp.float32,
                )
                for part in range(2)
            )
            place = pl.ds(b * items, items)
            if chunk > 0:
                total = total + field[place]
            if chunk < CHUNKS - 1:
                field[place] = total
            else:
                cube[place] = total.astype(jnp.bfloat16)

    margin = 8
    for d in range(per):
        series[d, :margin] = jnp.zeros((margin, TILE), jnp.float32)
        series[d, margin + intervals * blocks :] = jnp.zeros((margin, TILE), jnp.float32)

    batch = tiles.shape[0] // TILE

    def sample(first, place_in_batch):
        n = first + place_in_batch
        near = pl.multiple_of(place_in_batch * TILE, TILE)
        for d in range(per):
            terms = [
                jnp.take_along_axis(
                    tiles[pl.ds(near + b * blocks, blocks), d * TILE : (d + 1) * TILE],
                    shifts[n, b],
                    axis=1,
                    mode="promise_in_bounds",
                )
                * weights[n, b]
                for b in range(groups)
            ]
            total = jnp.zeros((blocks, TILE), jnp.float32)
            for k in range(groups):
                moved = terms[(groups - 1 - k) % groups]
                for t in range(groups - 1):
                    moved = jnp.where(group == t, terms[(t - k) % groups], moved)
                if k:
                    moved = pltpu.roll(moved, TILE - k * each, 1)
                total = total + moved
            place = pl.ds(pl.multiple_of(margin + n * blocks, 8), blocks)
            series[d, place] = total.astype(jnp.bfloat16).astype(jnp.float32)

    def out_copy(target, source):
        return pltpu.make_async_remote_copy(
            src_ref=signal_out.at[target],
            dst_ref=signal_in.at[source],
            send_sem=out_send.at[target],
            recv_sem=out_recv.at[source],
            device_id=(det, target),
            device_id_type=MESH,
        )

    def smooth(n):
        windows = []
        for d in range(per):
            near = series[d, pl.ds(pl.multiple_of(n * blocks, 8), blocks + 2 * margin)]
            windows.append(
                jnp.concatenate(
                    [near[margin + s : margin + s + blocks] for s in (-1, 0, 1)], axis=1
                )
            )
        window = jnp.concatenate(windows, axis=0).astype(jnp.bfloat16)
        smoothed = jnp.dot(window, band[0], preferred_element_type=jnp.float32) + jnp.dot(
            window, band[1], preferred_element_type=jnp.float32
        )
        return smoothed.astype(jnp.bfloat16).reshape(per, blocks, TILE)

    def finish(target):
        signal_out[target] = smooth(target)

        @pl.when(target != me)
        def _():
            out_copy(target, me).start()

    batches = intervals // batch
    origin = (me // batch + 1) * batch

    def one_batch(turn, carry):
        first = lax.rem(origin + turn * batch, intervals)
        chosen = picks[pl.ds(first, batch)].reshape(batch * TILE, -1)
        tiles[...] = jnp.dot(chosen, cube[...], preferred_element_type=jnp.float32)

        def each_sample(step, inner):
            sample(first, step)
            return inner

        lax.fori_loop(0, batch, each_sample, 0)

        def each_finish(step, inner):
            finish(lax.rem(first + intervals - 1 + step, intervals))
            return inner

        lax.fori_loop(jnp.where(turn == 0, 2, 0), batch, each_finish, 0)
        return carry

    lax.fori_loop(0, batches, one_batch, 0)
    finish(lax.rem(origin + intervals - 1, intervals))
    finish(lax.rem(origin, intervals))

    out_ref[me] = signal_out[me].astype(jnp.float32)

    def collect(step, carry):
        source = lax.rem(me + count - step, count)
        out_copy(source, source).wait_recv()
        out_ref[source] = signal_in[source].astype(jnp.float32)
        return carry

    lax.fori_loop(1, count, collect, 0)

    def drain(step, carry):
        target = lax.rem(me + step, count)
        info_copy(target, me).wait_send()
        for chunk in range(CHUNKS):
            spec_copy(chunk, target, me).wait_send()
        out_copy(target, me).wait_send()
        return carry

    lax.fori_loop(1, count, drain, 0)
    for chunk in range(CHUNKS):
        pair_copy(chunk).wait_send()
    share_copy.wait_send()


def local_fused(wigner, alm, beam, crossing, offsets, fraction, taps):
    det_count = lax.axis_size("det")
    count = lax.axis_size("ord")
    orders, beams, lats, depth = wigner.shape
    dets = beam.shape[0]
    per = dets // det_count // count
    orders_total = orders * count
    longitudes = 2 * orders_total
    groups = longitudes // TILE
    items = beams * lats
    tiles = items * groups
    intervals = count
    blocks = offsets.shape[1] // TILE
    chunk_rows = orders // CHUNKS * per * 2

    table = fourier_tables(orders_total, per).reshape(
        2, count, CHUNKS, chunk_rows, longitudes * per
    )
    table = jnp.asarray(
        np.swapaxes(table, 1, 2).reshape(2, CHUNKS, count * chunk_rows, longitudes * per)
    )

    f32, bf16 = jnp.float32, jnp.bfloat16
    dma = pltpu.SemaphoreType.DMA
    vmem = pl.BlockSpec(memory_space=pltpu.VMEM)
    anywhere = pl.BlockSpec(memory_space=pl.ANY)
    partial = pltpu.VMEM((CHUNKS, count, chunk_rows, items), f32)
    outgoing = pltpu.VMEM((CHUNKS, count, chunk_rows, items), bf16)
    arriving = pltpu.VMEM((count, CHUNKS, chunk_rows, items), bf16)
    result = pl.pallas_call(
        functools.partial(kernel, count, per, intervals, groups),
        out_shape=jax.ShapeDtypeStruct((count, per, blocks, TILE), f32),
        in_specs=[
            anywhere, anywhere, anywhere, anywhere, vmem, vmem, vmem,
            pl.BlockSpec(memory_space=pltpu.SMEM),
        ],
        out_specs=vmem,
        scratch_shapes=[
            pltpu.VMEM((dets * beams, depth), bf16),
            pltpu.VMEM((orders * 2, depth), bf16),
            pltpu.VMEM((beams, dets * 2, depth), bf16),
            pltpu.VMEM((orders, 16, depth), bf16),
            pltpu.VMEM(wigner.shape, bf16),
            pltpu.VMEM(table.shape, bf16),
            partial, partial, partial, outgoing, arriving,
            pltpu.VMEM((INFO_ROWS, TILE), f32),
            pltpu.VMEM((2, count, INFO_ROWS, TILE), f32),
            pltpu.VMEM((intervals, TILE, tiles), bf16),
            pltpu.VMEM((intervals, groups, blocks, TILE), jnp.int32),
            pltpu.VMEM((intervals, groups, blocks, TILE), f32),
            pltpu.VMEM((2, 3 * TILE, TILE), bf16),
            pltpu.VMEM((tiles, per * TILE), f32),
            pltpu.VMEM((tiles, per * TILE), bf16),
            pltpu.VMEM((BATCH * TILE, per * TILE), f32),
            pltpu.VMEM((per, intervals * blocks + 16, TILE), f32),
            pltpu.VMEM((count, per, blocks, TILE), bf16),
            pltpu.VMEM((count, per, blocks, TILE), bf16),
            dma((2,)), dma((CHUNKS,)), dma, dma((count,)), dma((count,)), dma, dma,
            dma((CHUNKS,)), dma((CHUNKS,)), dma((CHUNKS, count)), dma((CHUNKS, count)),
            dma((count,)), dma((count,)),
        ],
        compiler_params=pltpu.CompilerParams(
            collective_id=0, has_side_effects=True, vmem_limit_bytes=56 * 2**20
        ),
    )(
        wigner,
        beam.reshape(dets * beams, -1),
        alm.reshape(orders * 2, -1),
        table,
        crossing,
        offsets.reshape(blocks, TILE),
        fraction.reshape(blocks, TILE),
        taps,
    )
    return result.reshape(count * per, blocks * TILE)


def with_halo(cells, sides, width):
    for axis, dim in sides:
        count = lax.axis_size(axis)
        ends = count - 1
        head = lax.slice_in_dim(cells, 0, width, axis=dim)
        tail = lax.slice_in_dim(cells, cells.shape[dim] - width, cells.shape[dim], axis=dim)
        cells = jnp.concatenate(
            [
                lax.ppermute(tail, axis, [(i, (i + 1) % count) for i in range(ends)]),
                cells,
                lax.ppermute(head, axis, [((i + 1) % count, i) for i in range(ends)]),
            ],
            axis=dim,
        )
    return cells


def lagrange_weights(position):
    shifted = position + 1.0
    minus_one = position - 1.0
    minus_two = position - 2.0
    return (
        -position * minus_one * minus_two / 6.0,
        shifted * minus_one * minus_two / 2.0,
        -shifted * position * minus_two / 2.0,
        shifted * position * minus_one / 6.0,
    )


def stencil_matrix(offset_part, fraction_part, width):
    columns = jnp.arange(width, dtype=jnp.int32)
    distance = columns[:, None] - offset_part[..., None, :]
    factors = lagrange_weights(fraction_part[..., None, :])
    matrix = jnp.zeros(distance.shape, jnp.float32)
    for place in range(4):
        matrix = matrix + jnp.where(distance == place, factors[place], 0.0)
    return matrix


def sky_beam(alm_part, beam_part):
    product = (
        beam_part.astype(jnp.float32)[:, None, :, None, :]
        * alm_part.astype(jnp.float32)[None, :, None, :, :]
    )
    return product.astype(jnp.bfloat16)


def local(wigner, alm, beam, crossing, offsets, fraction, taps):
    det_count = lax.axis_size("det")
    det_index = lax.axis_index("det")
    ord_count = lax.axis_size("ord")
    orders_local = wigner.shape[0]
    half_width = wigner.shape[3]
    det_local = beam.shape[0] // det_count
    alm_half = lax.dynamic_slice_in_dim(alm, det_index * half_width, half_width, 2)
    beam_half = lax.dynamic_slice_in_dim(beam, det_index * half_width, half_width, 2)
    spectra = lax.psum_scatter(
        jnp.einsum(
            "mkrl,jmkcl->jkrcm",
            wigner,
            sky_beam(alm_half, beam_half),
            preferred_element_type=jnp.float32,
        ),
        "det",
        scatter_dimension=0,
        tiled=True,
    )
    items_all = wigner.shape[1] * wigner.shape[2]
    outgoing = spectra.astype(jnp.bfloat16).reshape(det_local, items_all, 2 * orders_local)
    arrived = lax.all_to_all(outgoing, "ord", split_axis=1, concat_axis=2, tiled=True)
    items_local = items_all // ord_count
    spectrum = arrived.reshape(det_local, items_local, ord_count, 2, orders_local).astype(
        jnp.float32
    )
    orders_total = ord_count * orders_local
    longitudes = 2 * orders_total
    block = math.gcd(512, longitudes)
    order_ids = (
        jnp.arange(ord_count, dtype=jnp.int32)[:, None] * orders_local
        + jnp.arange(orders_local, dtype=jnp.int32)[None, :]
    )
    weight_row = (jnp.where(order_ids == 0, 1.0, 2.0) / math.sqrt(longitudes))[:, :, None]
    step_angle = 2.0 * math.pi / longitudes
    base_phase = (
        order_ids[:, :, None] * jnp.arange(block, dtype=jnp.int32)[None, None, :] % longitudes
    )
    base_angle = base_phase.astype(jnp.float32) * step_angle
    base_cos = jnp.cos(base_angle)
    base_sin = jnp.sin(base_angle)
    pieces = []
    for first in range(0, longitudes, block):
        shift_angle = (order_ids * first % longitudes).astype(jnp.float32)[:, :, None] * step_angle
        shift_cos = jnp.cos(shift_angle)
        shift_sin = jnp.sin(shift_angle)
        cos_block = base_cos * shift_cos - base_sin * shift_sin
        sin_block = base_sin * shift_cos + base_cos * shift_sin
        table = jnp.stack([weight_row * cos_block, -weight_row * sin_block], axis=1)
        pieces.append(
            jnp.einsum("jincs,ncsp->ijp", spectrum, table, precision=lax.Precision.HIGHEST)
        )
    cube = jnp.concatenate(pieces, axis=2).astype(jnp.bfloat16)
    tile_width = TILE
    blocks_per_item = longitudes // tile_width
    tiles = cube.reshape(items_local, det_local, blocks_per_item, tile_width).transpose(0, 2, 1, 3)
    tiles = tiles.reshape(items_local * blocks_per_item, det_local, tile_width)
    tiles_local = tiles.shape[0]
    wanted = crossing[0]
    crossings = wanted.shape[0]
    capacity = max(2, 2 * crossings // ord_count)
    holder = wanted // tiles_local
    local_ids = wanted % tiles_local
    order_index = jnp.arange(crossings, dtype=jnp.int32)
    earlier = (holder[:, None] == holder[None, :]) & (order_index[None, :] < order_index[:, None])
    slot_ids = jnp.sum(earlier.astype(jnp.int32), axis=1)
    flat_slot = holder * capacity + slot_ids
    chosen = flat_slot[:, None] == jnp.arange(ord_count * capacity, dtype=jnp.int32)[None, :]
    requests = (jnp.sum(jnp.where(chosen, local_ids[:, None] + 1, 0), axis=0) - 1).reshape(
        ord_count, capacity
    )
    offset_rows = offsets[0].reshape(crossings, -1)
    fraction_rows = fraction[0].reshape(crossings, -1)
    samples_each = offset_rows.shape[1]
    slot_crossing = jnp.sum(jnp.where(chosen, order_index[:, None], 0), axis=0)
    occupied = jnp.any(chosen, axis=0)
    slot_offsets = jnp.where(occupied[:, None], offset_rows[slot_crossing], 0)
    slot_offsets = slot_offsets.reshape(ord_count, capacity, samples_each)
    slot_fractions = jnp.where(occupied[:, None], fraction_rows[slot_crossing], 0.0)
    slot_fractions = slot_fractions.reshape(ord_count, capacity, samples_each)
    asked = lax.all_to_all(requests, "ord", split_axis=0, concat_axis=0, tiled=True)
    asked_offsets = lax.all_to_all(slot_offsets, "ord", split_axis=0, concat_axis=0, tiled=True)
    asked_fractions = lax.all_to_all(slot_fractions, "ord", split_axis=0, concat_axis=0, tiled=True)
    stencil = stencil_matrix(asked_offsets, asked_fractions, tile_width)
    present = asked >= 0
    picked = tiles[jnp.maximum(asked, 0)]
    result = jnp.einsum(
        "rnjo,rnos->rnjs",
        jnp.where(present[..., None, None], picked, jnp.zeros((), jnp.bfloat16)).astype(
            jnp.float32
        ),
        stencil,
        precision=lax.Precision.HIGHEST,
    )
    received = lax.all_to_all(
        result.astype(jnp.bfloat16), "ord", split_axis=0, concat_axis=0, tiled=True
    )
    samples = jnp.transpose(received[holder, slot_ids], (1, 0, 2)).reshape(det_local, -1)
    reach = taps.shape[0] // 2
    extended = with_halo(samples, (("ord", 1),), reach)
    total_time = samples.shape[1]
    padded = jnp.concatenate(
        [extended, jnp.zeros((det_local, 128 - 2 * reach), jnp.bfloat16)], axis=1
    )
    windows = jnp.concatenate(
        [
            padded[:, :total_time].reshape(det_local, -1, 128),
            padded[:, 128 : total_time + 128].reshape(det_local, -1, 128),
        ],
        axis=2,
    )
    lag_index = (
        jnp.arange(256, dtype=jnp.int32)[:, None] - jnp.arange(128, dtype=jnp.int32)[None, :]
    )
    inside = (lag_index >= 0) & (lag_index < taps.shape[0])
    banded = jnp.where(inside, taps[jnp.clip(lag_index, 0, taps.shape[0] - 1)], 0.0)
    smoothed = jnp.einsum(
        "jbu,uo->jbo", windows.astype(jnp.float32), banded, precision=lax.Precision.HIGHEST
    )
    return smoothed.reshape(det_local, total_time)


def splits_detectors(mesh, wigner, beam, offsets):
    count = mesh.shape["ord"]
    return (
        mesh.shape["det"] == 2
        and beam.shape[0] == 4 * count
        and wigner.shape[0] == 4 * CHUNKS * count
        and 2 * wigner.shape[0] == 4 * TILE
        and wigner.shape[1:3] == (2, TILE)
        and offsets.shape == (count, 32 * TILE)
        and count % BATCH == 0
    )


def solution(mesh):
    def run(wigner, alm, beam, crossing, offsets, fraction, taps):
        fused = splits_detectors(mesh, wigner, beam, offsets)
        return jax.shard_map(
            local_fused if fused else local,
            mesh=mesh,
            in_specs=(
                P("ord", None, None, "det"),
                P("ord", None),
                P(),
                P("ord"),
                P("ord"),
                P("ord"),
                P(),
            ),
            out_specs=P("det", "ord"),
            check_vma=False,
        )(wigner, alm, beam, crossing, offsets, fraction, taps)

    return run
```

```python
import functools
import math

import jax
import jax.numpy as jnp
import numpy as np
from jax import lax
from jax.experimental import pallas as pl
from jax.experimental.pallas import tpu as pltpu
from jax.sharding import PartitionSpec as P

TILE = 128
CHUNKS = 4
PLANE = 4
BATCH = 4
INFO_ROWS = 40
MESH = pl.DeviceIdType.MESH


def split_parts(values):
    high = values.astype(jnp.bfloat16)
    return high, (values - high.astype(jnp.float32)).astype(jnp.bfloat16)


def fourier_tables(orders_total, per):
    longitudes = 2 * orders_total
    order = np.arange(orders_total, dtype=np.int64)
    phase = (order[:, None] * np.arange(longitudes)[None, :]) % longitudes
    angle = phase * (2.0 * math.pi / longitudes)
    weight = np.where(order == 0, 1.0, 2.0)[:, None] / math.sqrt(longitudes)
    parts = np.stack([weight * np.cos(angle), -weight * np.sin(angle)], axis=1)
    parts = parts.reshape(orders_total, 2, longitudes // TILE, TILE)
    table = np.zeros((orders_total, per, 2, longitudes // TILE, per, TILE), np.float32)
    for det in range(per):
        table[:, det, :, :, det, :] = parts
    table = table.reshape(orders_total * per * 2, longitudes * per)
    high = table.astype(jnp.bfloat16)
    low = (table - high.astype(np.float32)).astype(jnp.bfloat16)
    return np.stack([high, low])


def kernel(
    count, per, intervals, tiles_per_item,
    wigner_hbm, beam_hbm, alm_hbm, table_hbm, crossing_ref, offsets_ref, fraction_ref, taps_ref,
    out_ref,
    beam_in, alm_in, beam_ref, alm_ref,
    wigner, table, partial_own, partial_out, partial_in, spectra_out, spectra_in,
    info_ref, info, picks, shifts, weights, band, field, cube, tiles, series,
    signal_out, signal_in,
    small_sem, wigner_sem, table_sem, info_send, info_recv, column_send, column_recv, share_send, share_recv,
    pair_send, pair_recv, spec_send, spec_recv, out_send, out_recv,
):
    det = lax.axis_index("det")
    me = lax.axis_index("ord")
    partner = 1 - det
    orders = wigner.shape[0]
    chunk_orders = orders // CHUNKS
    blocks = shifts.shape[2]
    groups = tiles_per_item

    def wigner_copy(chunk):
        part = pl.ds(chunk * chunk_orders, chunk_orders)
        return pltpu.make_async_copy(wigner_hbm.at[part], wigner.at[part], wigner_sem.at[chunk])

    depth = beam_in.shape[2]
    near_depth = pl.ds(pl.multiple_of(det * depth, TILE), depth)
    beam_copy = pltpu.make_async_copy(beam_hbm.at[:, :, near_depth], beam_in, small_sem.at[0])
    alm_copy = pltpu.make_async_copy(alm_hbm.at[:, :, near_depth], alm_in, small_sem.at[1])
    beam_copy.start()
    alm_copy.start()
    for chunk in range(CHUNKS):
        wigner_copy(chunk).start()
    table_copy = pltpu.make_async_copy(table_hbm, table, table_sem)
    table_copy.start()

    barrier = pltpu.get_barrier_semaphore()

    def greet(step, carry):
        peer = lax.rem(me + step, count)
        pl.semaphore_signal(barrier, inc=1, device_id=(det, peer), device_id_type=MESH)
        return carry

    lax.fori_loop(1, count, greet, 0)
    pl.semaphore_signal(barrier, inc=1, device_id=(partner, me), device_id_type=MESH)

    def select_rows(source, wanted_column):
        chosen = jnp.where(
            wanted_column == lax.broadcasted_iota(jnp.int32, wanted_column.shape, 1), 1.0, 0.0
        ).astype(jnp.bfloat16)
        return jnp.dot(chosen, source, preferred_element_type=jnp.float32).astype(jnp.bfloat16)

    beams = wigner.shape[1]
    beam_copy.wait()
    beam_rows_all = beam_ref.shape[1]
    beam_source = beam_in[...].reshape(-1, depth)
    row = lax.broadcasted_iota(jnp.int32, (beam_rows_all, beam_source.shape[0]), 0)
    half_rows = beam_rows_all // 2
    side = lax.rem(row // half_rows + det, 2)
    beam_column = (side * (half_rows // 2) + row % half_rows // 2) * beams
    for beam_order in range(beams):
        beam_ref[beam_order] = select_rows(beam_source, beam_column + beam_order)
    alm_copy.wait()
    repeat = alm_ref.shape[1]
    alm_source = alm_in[...].reshape(-1, depth)
    row = lax.broadcasted_iota(jnp.int32, (orders * repeat, alm_source.shape[0]), 0)
    alm_ref[...] = select_rows(alm_source, row // repeat * 2 + row % 2).reshape(
        alm_ref.shape
    )

    half_blocks = blocks // 2
    near_blocks = pl.ds(pl.multiple_of(det * half_blocks, 8), half_blocks)
    info_ref[:half_blocks] = offsets_ref[near_blocks].astype(jnp.float32)
    info_ref[half_blocks : 2 * half_blocks] = fraction_ref[near_blocks]
    ids = jnp.broadcast_to(crossing_ref[...], (8, TILE))
    ids = ids % groups * (cube.shape[0] // groups) + ids // groups
    lanes_row = lax.broadcasted_iota(jnp.int32, (8, TILE), 1)
    info_ref[2 * half_blocks :] = jnp.take_along_axis(
        ids.astype(jnp.float32),
        lanes_row % blocks * groups + lanes_row // blocks,
        axis=1,
        mode="promise_in_bounds",
    )

    planes = count // PLANE
    near, plane = lax.rem(me, PLANE), me // PLANE

    def info_copy(step):
        return pltpu.make_async_remote_copy(
            src_ref=info_ref,
            dst_ref=info.at[det, near, plane],
            send_sem=info_send,
            recv_sem=info_recv,
            device_id=(det, lax.rem(me + step * PLANE, count)),
            device_id_type=MESH,
        )

    def column_copy(step):
        return pltpu.make_async_remote_copy(
            src_ref=info.at[det, near],
            dst_ref=info.at[det, near],
            send_sem=column_send,
            recv_sem=column_recv,
            device_id=(det, plane * PLANE + lax.rem(near + step, PLANE)),
            device_id_type=MESH,
        )

    def await_bytes(block, semaphore):
        pltpu.make_async_copy(block, block, semaphore).wait()

    rows = per * 2
    own_rows = count * rows

    def product(order, beam_order):
        alm_rows = alm_ref[order]
        beam_rows = beam_ref[beam_order]
        sky = beam_rows.reshape(-1, alm_rows.shape[0], depth) * alm_rows[None]
        return lax.dot_general(
            sky.reshape(-1, depth),
            wigner[order, beam_order],
            (((1,), (1,)), ((), ())),
            preferred_element_type=jnp.float32,
        )

    def multiply(chunk):
        wigner_copy(chunk).wait()

        def pair(step, carry):
            first = chunk * chunk_orders + 2 * step
            place = pl.ds(pl.multiple_of(step * 2 * rows, 2 * rows), 2 * rows)
            for beam_order in range(wigner.shape[1]):
                lanes = pl.ds(beam_order * wigner.shape[2], wigner.shape[2])
                one = product(first, beam_order)
                two = product(first + 1, beam_order)
                for target, low in ((partial_own, 0), (partial_out, own_rows)):
                    target[chunk, :, place, lanes] = jnp.concatenate(
                        [
                            one[low : low + own_rows].reshape(count, rows, -1),
                            two[low : low + own_rows].reshape(count, rows, -1),
                        ],
                        axis=1,
                    )
            return carry

        lax.fori_loop(0, chunk_orders // 2, pair, 0)

    def pair_copy(chunk):
        return pltpu.make_async_remote_copy(
            src_ref=partial_out.at[chunk],
            dst_ref=partial_in.at[chunk],
            send_sem=pair_send.at[chunk],
            recv_sem=pair_recv.at[chunk],
            device_id=(partner, me),
            device_id_type=MESH,
        )

    def spec_copy(chunk, target, source):
        return pltpu.make_async_remote_copy(
            src_ref=spectra_out.at[chunk, target],
            dst_ref=spectra_in.at[source, chunk],
            send_sem=spec_send.at[chunk],
            recv_sem=spec_recv.at[chunk],
            device_id=(det, target),
            device_id_type=MESH,
        )

    def spread(chunk):
        pair_copy(chunk).wait_recv()
        total = (partial_own[chunk] + partial_in[chunk]).astype(jnp.bfloat16)
        spectra_out[chunk] = total

        for step in range(count - 1):
            spec_copy(chunk, lax.rem(me + 1 + (step + PLANE - 1) % (count - 1), count), me).start()
        spectra_in[me, chunk] = spectra_out[chunk, me]

    for chunk in range(CHUNKS):
        multiply(chunk)
        if chunk == 0:
            pl.semaphore_wait(barrier, count)
            info[det, near, plane] = info_ref[...]
            for step in range(1, planes):
                info_copy(step).start()
        pair_copy(chunk).start()
        if chunk > 0:
            spread(chunk - 1)
        if chunk == CHUNKS // 2:
            await_bytes(info.at[det, near, pl.ds(0, planes - 1)], info_recv)
            for step in range(1, PLANE):
                column_copy(step).start()
    spread(CHUNKS - 1)

    await_bytes(info.at[det, pl.ds(0, PLANE - 1)], column_recv)
    share_copy = pltpu.make_async_remote_copy(
        src_ref=info.at[det],
        dst_ref=info.at[det],
        send_sem=share_send,
        recv_sem=share_recv,
        device_id=(partner, me),
        device_id_type=MESH,
    )
    share_copy.start()

    shape = (2 * TILE, TILE)
    place = lax.broadcasted_iota(jnp.int32, shape, 0)
    place = jnp.where(place < 3 * TILE // 2, place, place - 2 * TILE)
    lag = place - lax.broadcasted_iota(jnp.int32, shape, 1)
    reach = taps_ref.shape[0] // 2

    def add_tap(place, total):
        return jnp.where(lag == place - reach, taps_ref[place], total)

    band_values = lax.fori_loop(0, taps_ref.shape[0], add_tap, jnp.zeros(shape, jnp.float32))
    band_high, band_low = split_parts(band_values)
    band[:, :TILE] = band_high
    band[:, TILE:] = band_low

    pltpu.make_async_remote_copy(
        src_ref=info.at[partner],
        dst_ref=info.at[partner],
        send_sem=share_send,
        recv_sem=share_recv,
        device_id=(partner, me),
        device_id_type=MESH,
    ).wait_recv()

    lane = lax.broadcasted_iota(jnp.int32, (blocks, TILE), 1)
    each = TILE // groups
    group = lane // each
    items = cube.shape[0] // groups
    half_rows = blocks // 2

    def prepare(n, carry):
        wanted = info[0, n % PLANE, n // PLANE, 2 * half_rows : 2 * half_rows + 1, :]
        ids = jnp.broadcast_to(wanted, (TILE, TILE)).T
        for part in range(cube.shape[0] // TILE):
            places = lax.broadcasted_iota(jnp.int32, (TILE, TILE), 1) + part * TILE
            picks[n, :, part * TILE : (part + 1) * TILE] = jnp.where(
                ids == places.astype(jnp.float32), 1.0, 0.0
            ).astype(jnp.bfloat16)
        offset = jnp.concatenate([info[0, n % PLANE, n // PLANE, :half_rows], info[1, n % PLANE, n // PLANE, :half_rows]], axis=0)
        fraction = jnp.concatenate(
            [info[0, n % PLANE, n // PLANE, half_rows : 2 * half_rows], info[1, n % PLANE, n // PLANE, half_rows : 2 * half_rows]],
            axis=0,
        )
        for b in range(groups):
            spot = b * each + lane % each
            start = jnp.take_along_axis(offset, spot, axis=1, mode="promise_in_bounds")
            f = jnp.take_along_axis(fraction, spot, axis=1, mode="promise_in_bounds")
            shifts[n, b] = start.astype(jnp.int32) + group
            weights[n, b] = (
                jnp.where(group == 0, -1.0 / 6.0, f + 1.0)
                * jnp.where(group == 1, 0.5, f)
                * jnp.where(group == 2, -0.5, f - 1.0)
                * jnp.where(group == 3, 1.0 / 6.0, f - 2.0)
            )
        return carry

    lax.fori_loop(0, intervals, prepare, 0)

    table_copy.wait()
    chunk_rows = spectra_in.shape[2]
    for chunk in range(CHUNKS):
        await_bytes(spectra_in.at[pl.ds(0, count - 1), chunk], spec_recv.at[chunk])
        spectra = spectra_in[:, chunk].reshape(count * chunk_rows, items)
        for b in range(groups):
            columns = pl.ds(b * per * TILE, per * TILE)
            total = sum(
                lax.dot_general(
                    spectra,
                    table[part, chunk, :, columns],
                    (((0,), (0,)), ((), ())),
                    preferred_element_type=jnp.float32,
                )
                for part in range(2)
            )
            place = pl.ds(b * items, items)
            if chunk > 0:
                total = total + field[place]
            if chunk < CHUNKS - 1:
                field[place] = total
            else:
                cube[place] = total.astype(jnp.bfloat16)

    margin = 8
    for d in range(per):
        series[d, :margin] = jnp.zeros((margin, TILE), jnp.float32)
        series[d, margin + intervals * blocks :] = jnp.zeros((margin, TILE), jnp.float32)

    batch = tiles.shape[0] // TILE

    def sample(first, place_in_batch):
        n = first + place_in_batch
        near = pl.multiple_of(place_in_batch * TILE, TILE)
        for d in range(per):
            terms = [
                jnp.take_along_axis(
                    tiles[pl.ds(near + b * blocks, blocks), d * TILE : (d + 1) * TILE],
                    shifts[n, b],
                    axis=1,
                    mode="promise_in_bounds",
                )
                * weights[n, b]
                for b in range(groups)
            ]
            total = jnp.zeros((blocks, TILE), jnp.float32)
            for k in range(groups):
                moved = terms[(groups - 1 - k) % groups]
                for t in range(groups - 1):
                    moved = jnp.where(group == t, terms[(t - k) % groups], moved)
                if k:
                    moved = pltpu.roll(moved, TILE - k * each, 1)
                total = total + moved
            place = pl.ds(pl.multiple_of(margin + n * blocks, 8), blocks)
            series[d, place] = total.astype(jnp.bfloat16).astype(jnp.float32)

    def out_copy(target, source):
        return pltpu.make_async_remote_copy(
            src_ref=signal_out.at[target],
            dst_ref=signal_in.at[source],
            send_sem=out_send,
            recv_sem=out_recv.at[source],
            device_id=(det, target),
            device_id_type=MESH,
        )

    def smooth(n):
        windows = []
        for d in range(per):
            rows_near = series[d, pl.ds(pl.multiple_of(n * blocks, 8), blocks + 2 * margin)]
            before, here, after = (
                rows_near[margin + s : margin + s + blocks] for s in (-1, 0, 1)
            )
            sides = jnp.where(lane < TILE // 2, after, before)
            windows.append(jnp.concatenate([here, sides], axis=1))
        window = jnp.concatenate(windows, axis=0).astype(jnp.bfloat16)
        both = jnp.dot(window, band[...], preferred_element_type=jnp.float32)
        smoothed = both[:, :TILE] + both[:, TILE:]
        return smoothed.astype(jnp.bfloat16).reshape(per, blocks, TILE)

    def finish(target):
        signal_out[target] = smooth(target)

        @pl.when(target != me)
        def _():
            out_copy(target, me).start()

    batches = intervals // batch
    origin = (me // batch + 1) * batch

    def one_batch(turn, carry):
        first = lax.rem(origin + turn * batch, intervals)
        chosen = picks[pl.ds(first, batch)].reshape(batch * TILE, -1)
        tiles[...] = jnp.dot(chosen, cube[...], preferred_element_type=jnp.float32)

        def each_sample(step, inner):
            sample(first, step)
            return inner

        lax.fori_loop(0, batch, each_sample, 0)

        def each_finish(step, inner):
            finish(lax.rem(first + intervals - 1 + step, intervals))
            return inner

        lax.fori_loop(jnp.where(turn == 0, 2, 0), batch, each_finish, 0)
        return carry

    lax.fori_loop(0, batches, one_batch, 0)
    finish(lax.rem(origin + intervals - 1, intervals))
    finish(lax.rem(origin, intervals))

    signal_in[me] = signal_out[me]
    for source in range(count):
        @pl.when(source != me)
        def _(source=source):
            out_copy(source, source).wait_recv()

        for d in range(per):
            values = signal_in[source, d].astype(jnp.float32)
            row = source * per + d
            for block in range(blocks):
                out_ref[row : row + 1, block * TILE : (block + 1) * TILE] = values[
                    block : block + 1
                ]

    await_bytes(info.at[det, near, pl.ds(0, planes - 1)], info_send)
    await_bytes(info.at[det, pl.ds(0, PLANE - 1)], column_send)
    await_bytes(signal_out.at[pl.ds(0, count - 1)], out_send)
    for chunk in range(CHUNKS):
        await_bytes(spectra_out.at[chunk, pl.ds(0, count - 1)], spec_send.at[chunk])
    for chunk in range(CHUNKS):
        pair_copy(chunk).wait_send()
    share_copy.wait_send()


def local_fused(wigner, alm, beam, crossing, offsets, fraction, taps):
    det_count = lax.axis_size("det")
    count = lax.axis_size("ord")
    orders, beams, lats, depth = wigner.shape
    dets = beam.shape[0]
    per = dets // det_count // count
    orders_total = orders * count
    longitudes = 2 * orders_total
    groups = longitudes // TILE
    items = beams * lats
    tiles = items * groups
    intervals = count
    blocks = offsets.shape[1] // TILE
    chunk_rows = orders // CHUNKS * per * 2

    table = fourier_tables(orders_total, per).reshape(
        2, count, CHUNKS, chunk_rows, longitudes * per
    )
    table = jnp.asarray(
        np.swapaxes(table, 1, 2).reshape(2, CHUNKS, count * chunk_rows, longitudes * per)
    )

    f32, bf16 = jnp.float32, jnp.bfloat16
    dma = pltpu.SemaphoreType.DMA
    vmem = pl.BlockSpec(memory_space=pltpu.VMEM)
    anywhere = pl.BlockSpec(memory_space=pl.ANY)
    partial = pltpu.VMEM((CHUNKS, count, chunk_rows, items), f32)
    outgoing = pltpu.VMEM((CHUNKS, count, chunk_rows, items), bf16)
    arriving = pltpu.VMEM((count, CHUNKS, chunk_rows, items), bf16)
    result = pl.pallas_call(
        functools.partial(kernel, count, per, intervals, groups),
        out_shape=jax.ShapeDtypeStruct((count * per, blocks * TILE), f32),
        in_specs=[
            anywhere, anywhere, anywhere, anywhere, vmem, vmem, vmem,
            pl.BlockSpec(memory_space=pltpu.SMEM),
        ],
        out_specs=vmem,
        scratch_shapes=[
            pltpu.VMEM((dets, beams, depth), bf16),
            pltpu.VMEM((orders, 2, depth), bf16),
            pltpu.VMEM((beams, dets * 2, depth), bf16),
            pltpu.VMEM((orders, 16, depth), bf16),
            pltpu.VMEM(wigner.shape, bf16),
            pltpu.VMEM(table.shape, bf16),
            partial, partial, partial, outgoing, arriving,
            pltpu.VMEM((INFO_ROWS, TILE), f32),
            pltpu.VMEM((2, PLANE, count // PLANE, INFO_ROWS, TILE), f32),
            pltpu.VMEM((intervals, TILE, tiles), bf16),
            pltpu.VMEM((intervals, groups, blocks, TILE), jnp.int32),
            pltpu.VMEM((intervals, groups, blocks, TILE), f32),
            pltpu.VMEM((2 * TILE, 2 * TILE), bf16),
            pltpu.VMEM((tiles, per * TILE), f32),
            pltpu.VMEM((tiles, per * TILE), bf16),
            pltpu.VMEM((BATCH * TILE, per * TILE), f32),
            pltpu.VMEM((per, intervals * blocks + 16, TILE), f32),
            pltpu.VMEM((count, per, blocks, TILE), bf16),
            pltpu.VMEM((count, per, blocks, TILE), bf16),
            dma((2,)), dma((CHUNKS,)), dma, dma, dma, dma, dma, dma, dma,
            dma((CHUNKS,)), dma((CHUNKS,)), dma((CHUNKS,)), dma((CHUNKS,)),
            dma, dma((count,)),
        ],
        compiler_params=pltpu.CompilerParams(
            collective_id=0, has_side_effects=True, vmem_limit_bytes=56 * 2**20
        ),
    )(
        wigner,
        beam,
        alm,
        table,
        crossing,
        offsets.reshape(blocks, TILE),
        fraction.reshape(blocks, TILE),
        taps,
    )
    return result


def with_halo(cells, sides, width):
    for axis, dim in sides:
        count = lax.axis_size(axis)
        ends = count - 1
        head = lax.slice_in_dim(cells, 0, width, axis=dim)
        tail = lax.slice_in_dim(cells, cells.shape[dim] - width, cells.shape[dim], axis=dim)
        cells = jnp.concatenate(
            [
                lax.ppermute(tail, axis, [(i, (i + 1) % count) for i in range(ends)]),
                cells,
                lax.ppermute(head, axis, [((i + 1) % count, i) for i in range(ends)]),
            ],
            axis=dim,
        )
    return cells


def lagrange_weights(position):
    shifted = position + 1.0
    minus_one = position - 1.0
    minus_two = position - 2.0
    return (
        -position * minus_one * minus_two / 6.0,
        shifted * minus_one * minus_two / 2.0,
        -shifted * position * minus_two / 2.0,
        shifted * position * minus_one / 6.0,
    )


def stencil_matrix(offset_part, fraction_part, width):
    columns = jnp.arange(width, dtype=jnp.int32)
    distance = columns[:, None] - offset_part[..., None, :]
    factors = lagrange_weights(fraction_part[..., None, :])
    matrix = jnp.zeros(distance.shape, jnp.float32)
    for place in range(4):
        matrix = matrix + jnp.where(distance == place, factors[place], 0.0)
    return matrix


def sky_beam(alm_part, beam_part):
    product = (
        beam_part.astype(jnp.float32)[:, None, :, None, :]
        * alm_part.astype(jnp.float32)[None, :, None, :, :]
    )
    return product.astype(jnp.bfloat16)


def local(wigner, alm, beam, crossing, offsets, fraction, taps):
    det_count = lax.axis_size("det")
    det_index = lax.axis_index("det")
    ord_count = lax.axis_size("ord")
    orders_local = wigner.shape[0]
    half_width = wigner.shape[3]
    det_local = beam.shape[0] // det_count
    alm_half = lax.dynamic_slice_in_dim(alm, det_index * half_width, half_width, 2)
    beam_half = lax.dynamic_slice_in_dim(beam, det_index * half_width, half_width, 2)
    spectra = lax.psum_scatter(
        jnp.einsum(
            "mkrl,jmkcl->jkrcm",
            wigner,
            sky_beam(alm_half, beam_half),
            preferred_element_type=jnp.float32,
        ),
        "det",
        scatter_dimension=0,
        tiled=True,
    )
    items_all = wigner.shape[1] * wigner.shape[2]
    outgoing = spectra.astype(jnp.bfloat16).reshape(det_local, items_all, 2 * orders_local)
    arrived = lax.all_to_all(outgoing, "ord", split_axis=1, concat_axis=2, tiled=True)
    items_local = items_all // ord_count
    spectrum = arrived.reshape(det_local, items_local, ord_count, 2, orders_local).astype(
        jnp.float32
    )
    orders_total = ord_count * orders_local
    longitudes = 2 * orders_total
    block = math.gcd(512, longitudes)
    order_ids = (
        jnp.arange(ord_count, dtype=jnp.int32)[:, None] * orders_local
        + jnp.arange(orders_local, dtype=jnp.int32)[None, :]
    )
    weight_row = (jnp.where(order_ids == 0, 1.0, 2.0) / math.sqrt(longitudes))[:, :, None]
    step_angle = 2.0 * math.pi / longitudes
    base_phase = (
        order_ids[:, :, None] * jnp.arange(block, dtype=jnp.int32)[None, None, :] % longitudes
    )
    base_angle = base_phase.astype(jnp.float32) * step_angle
    base_cos = jnp.cos(base_angle)
    base_sin = jnp.sin(base_angle)
    pieces = []
    for first in range(0, longitudes, block):
        shift_angle = (order_ids * first % longitudes).astype(jnp.float32)[:, :, None] * step_angle
        shift_cos = jnp.cos(shift_angle)
        shift_sin = jnp.sin(shift_angle)
        cos_block = base_cos * shift_cos - base_sin * shift_sin
        sin_block = base_sin * shift_cos + base_cos * shift_sin
        table = jnp.stack([weight_row * cos_block, -weight_row * sin_block], axis=1)
        pieces.append(
            jnp.einsum("jincs,ncsp->ijp", spectrum, table, precision=lax.Precision.HIGHEST)
        )
    cube = jnp.concatenate(pieces, axis=2).astype(jnp.bfloat16)
    tile_width = TILE
    blocks_per_item = longitudes // tile_width
    tiles = cube.reshape(items_local, det_local, blocks_per_item, tile_width).transpose(0, 2, 1, 3)
    tiles = tiles.reshape(items_local * blocks_per_item, det_local, tile_width)
    tiles_local = tiles.shape[0]
    wanted = crossing[0]
    crossings = wanted.shape[0]
    capacity = max(2, 2 * crossings // ord_count)
    holder = wanted // tiles_local
    local_ids = wanted % tiles_local
    order_index = jnp.arange(crossings, dtype=jnp.int32)
    earlier = (holder[:, None] == holder[None, :]) & (order_index[None, :] < order_index[:, None])
    slot_ids = jnp.sum(earlier.astype(jnp.int32), axis=1)
    flat_slot = holder * capacity + slot_ids
    chosen = flat_slot[:, None] == jnp.arange(ord_count * capacity, dtype=jnp.int32)[None, :]
    requests = (jnp.sum(jnp.where(chosen, local_ids[:, None] + 1, 0), axis=0) - 1).reshape(
        ord_count, capacity
    )
    offset_rows = offsets[0].reshape(crossings, -1)
    fraction_rows = fraction[0].reshape(crossings, -1)
    samples_each = offset_rows.shape[1]
    slot_crossing = jnp.sum(jnp.where(chosen, order_index[:, None], 0), axis=0)
    occupied = jnp.any(chosen, axis=0)
    slot_offsets = jnp.where(occupied[:, None], offset_rows[slot_crossing], 0)
    slot_offsets = slot_offsets.reshape(ord_count, capacity, samples_each)
    slot_fractions = jnp.where(occupied[:, None], fraction_rows[slot_crossing], 0.0)
    slot_fractions = slot_fractions.reshape(ord_count, capacity, samples_each)
    asked = lax.all_to_all(requests, "ord", split_axis=0, concat_axis=0, tiled=True)
    asked_offsets = lax.all_to_all(slot_offsets, "ord", split_axis=0, concat_axis=0, tiled=True)
    asked_fractions = lax.all_to_all(slot_fractions, "ord", split_axis=0, concat_axis=0, tiled=True)
    stencil = stencil_matrix(asked_offsets, asked_fractions, tile_width)
    present = asked >= 0
    picked = tiles[jnp.maximum(asked, 0)]
    result = jnp.einsum(
        "rnjo,rnos->rnjs",
        jnp.where(present[..., None, None], picked, jnp.zeros((), jnp.bfloat16)).astype(
            jnp.float32
        ),
        stencil,
        precision=lax.Precision.HIGHEST,
    )
    received = lax.all_to_all(
        result.astype(jnp.bfloat16), "ord", split_axis=0, concat_axis=0, tiled=True
    )
    samples = jnp.transpose(received[holder, slot_ids], (1, 0, 2)).reshape(det_local, -1)
    reach = taps.shape[0] // 2
    extended = with_halo(samples, (("ord", 1),), reach)
    total_time = samples.shape[1]
    padded = jnp.concatenate(
        [extended, jnp.zeros((det_local, 128 - 2 * reach), jnp.bfloat16)], axis=1
    )
    windows = jnp.concatenate(
        [
            padded[:, :total_time].reshape(det_local, -1, 128),
            padded[:, 128 : total_time + 128].reshape(det_local, -1, 128),
        ],
        axis=2,
    )
    lag_index = (
        jnp.arange(256, dtype=jnp.int32)[:, None] - jnp.arange(128, dtype=jnp.int32)[None, :]
    )
    inside = (lag_index >= 0) & (lag_index < taps.shape[0])
    banded = jnp.where(inside, taps[jnp.clip(lag_index, 0, taps.shape[0] - 1)], 0.0)
    smoothed = jnp.einsum(
        "jbu,uo->jbo", windows.astype(jnp.float32), banded, precision=lax.Precision.HIGHEST
    )
    return smoothed.reshape(det_local, total_time)


def splits_detectors(mesh, wigner, beam, offsets):
    count = mesh.shape["ord"]
    return (
        mesh.shape["det"] == 2
        and beam.shape[0] == 4 * count
        and wigner.shape[0] == 4 * CHUNKS * count
        and 2 * wigner.shape[0] == 4 * TILE
        and wigner.shape[1:3] == (2, TILE)
        and offsets.shape == (count, 32 * TILE)
        and count % BATCH == 0
        and count % PLANE == 0
    )


def solution(mesh):
    def run(wigner, alm, beam, crossing, offsets, fraction, taps):
        fused = splits_detectors(mesh, wigner, beam, offsets)
        return jax.shard_map(
            local_fused if fused else local,
            mesh=mesh,
            in_specs=(
                P("ord", None, None, "det"),
                P("ord", None),
                P(),
                P("ord"),
                P("ord"),
                P("ord"),
                P(),
            ),
            out_specs=P("det", "ord"),
            check_vma=False,
        )(wigner, alm, beam, crossing, offsets, fraction, taps)

    return run
```

```python
import functools
import math

import jax
import jax.numpy as jnp
import numpy as np
from jax import lax
from jax.experimental import pallas as pl
from jax.experimental.pallas import tpu as pltpu
from jax.sharding import PartitionSpec as P

TILE = 128
CHUNKS = 4
PLANE = 4
BATCH = 4
INFO_ROWS = 40
MESH = pl.DeviceIdType.MESH


def split_parts(values):
    high = values.astype(jnp.bfloat16)
    return high, (values - high.astype(jnp.float32)).astype(jnp.bfloat16)


def fourier_tables(orders_total, per):
    longitudes = 2 * orders_total
    order = np.arange(orders_total, dtype=np.int64)
    phase = (order[:, None] * np.arange(longitudes)[None, :]) % longitudes
    angle = phase * (2.0 * math.pi / longitudes)
    weight = np.where(order == 0, 1.0, 2.0)[:, None] / math.sqrt(longitudes)
    parts = np.stack([weight * np.cos(angle), -weight * np.sin(angle)], axis=1)
    parts = parts.reshape(orders_total, 2, longitudes // TILE, TILE)
    table = np.zeros((orders_total, per, 2, longitudes // TILE, per, TILE), np.float32)
    for det in range(per):
        table[:, det, :, :, det, :] = parts
    table = table.reshape(orders_total * per * 2, longitudes * per)
    high = table.astype(jnp.bfloat16)
    low = (table - high.astype(np.float32)).astype(jnp.bfloat16)
    return np.stack([high, low])


def kernel(
    count, per, intervals, tiles_per_item,
    wigner_hbm, beam_hbm, alm_hbm, table_hbm, crossing_ref, offsets_ref, fraction_ref, taps_ref,
    out_ref,
    beam_in, alm_in, beam_ref, alm_ref,
    wigner, table, partial_own, partial_out, partial_in, spectra_out, spectra_in,
    info_ref, info, picks, shifts, weights, band, field, cube, tiles, series,
    signal_out, signal_in, wide,
    small_sem, wigner_sem, table_sem, info_send, info_recv, column_send, column_recv, share_send, share_recv,
    pair_send, pair_recv, spec_send, spec_recv, out_send, out_recv,
):
    det = lax.axis_index("det")
    me = lax.axis_index("ord")
    partner = 1 - det
    orders = wigner.shape[0]
    chunk_orders = orders // CHUNKS
    blocks = shifts.shape[2]
    groups = tiles_per_item

    def wigner_copy(chunk):
        part = pl.ds(chunk * chunk_orders, chunk_orders)
        return pltpu.make_async_copy(wigner_hbm.at[part], wigner.at[part], wigner_sem.at[chunk])

    depth = beam_in.shape[2]
    near_depth = pl.ds(pl.multiple_of(det * depth, TILE), depth)
    beam_copy = pltpu.make_async_copy(beam_hbm.at[:, :, near_depth], beam_in, small_sem.at[0])
    alm_copy = pltpu.make_async_copy(alm_hbm.at[:, :, near_depth], alm_in, small_sem.at[1])
    beam_copy.start()
    alm_copy.start()
    for chunk in range(CHUNKS):
        wigner_copy(chunk).start()
    table_copy = pltpu.make_async_copy(table_hbm, table, table_sem)
    table_copy.start()

    barrier = pltpu.get_barrier_semaphore()

    def greet(step, carry):
        peer = lax.rem(me + step, count)
        pl.semaphore_signal(barrier, inc=1, device_id=(det, peer), device_id_type=MESH)
        return carry

    lax.fori_loop(1, count, greet, 0)
    pl.semaphore_signal(barrier, inc=1, device_id=(partner, me), device_id_type=MESH)

    def select_rows(source, wanted_column):
        chosen = jnp.where(
            wanted_column == lax.broadcasted_iota(jnp.int32, wanted_column.shape, 1), 1.0, 0.0
        ).astype(jnp.bfloat16)
        return jnp.dot(chosen, source, preferred_element_type=jnp.float32).astype(jnp.bfloat16)

    beams = wigner.shape[1]
    beam_copy.wait()
    beam_rows_all = beam_ref.shape[1]
    beam_source = beam_in[...].reshape(-1, depth)
    row = lax.broadcasted_iota(jnp.int32, (beam_rows_all, beam_source.shape[0]), 0)
    half_rows = beam_rows_all // 2
    side = lax.rem(row // half_rows + det, 2)
    beam_column = (side * (half_rows // 2) + row % half_rows // 2) * beams
    for beam_order in range(beams):
        beam_ref[beam_order] = select_rows(beam_source, beam_column + beam_order)
    alm_copy.wait()
    repeat = alm_ref.shape[1]
    alm_source = alm_in[...].reshape(-1, depth)
    row = lax.broadcasted_iota(jnp.int32, (orders * repeat, alm_source.shape[0]), 0)
    alm_ref[...] = select_rows(alm_source, row // repeat * 2 + row % 2).reshape(
        alm_ref.shape
    )

    half_blocks = blocks // 2
    near_blocks = pl.ds(pl.multiple_of(det * half_blocks, 8), half_blocks)
    info_ref[:half_blocks] = offsets_ref[near_blocks].astype(jnp.float32)
    info_ref[half_blocks : 2 * half_blocks] = fraction_ref[near_blocks]
    ids = jnp.broadcast_to(crossing_ref[...], (8, TILE))
    ids = ids % groups * (cube.shape[0] // groups) + ids // groups
    lanes_row = lax.broadcasted_iota(jnp.int32, (8, TILE), 1)
    info_ref[2 * half_blocks :] = jnp.take_along_axis(
        ids.astype(jnp.float32),
        lanes_row % blocks * groups + lanes_row // blocks,
        axis=1,
        mode="promise_in_bounds",
    )

    planes = count // PLANE
    near, plane = lax.rem(me, PLANE), me // PLANE

    def info_copy(step):
        return pltpu.make_async_remote_copy(
            src_ref=info_ref,
            dst_ref=info.at[det, near, plane],
            send_sem=info_send,
            recv_sem=info_recv,
            device_id=(det, lax.rem(me + step * PLANE, count)),
            device_id_type=MESH,
        )

    def column_copy(step):
        return pltpu.make_async_remote_copy(
            src_ref=info.at[det, near],
            dst_ref=info.at[det, near],
            send_sem=column_send,
            recv_sem=column_recv,
            device_id=(det, plane * PLANE + lax.rem(near + step, PLANE)),
            device_id_type=MESH,
        )

    def await_bytes(block, semaphore):
        pltpu.make_async_copy(block, block, semaphore).wait()

    rows = per * 2
    own_rows = count * rows

    def product(order, beam_order):
        alm_rows = alm_ref[order]
        beam_rows = beam_ref[beam_order]
        sky = beam_rows.reshape(-1, alm_rows.shape[0], depth) * alm_rows[None]
        return lax.dot_general(
            sky.reshape(-1, depth),
            wigner[order, beam_order],
            (((1,), (1,)), ((), ())),
            preferred_element_type=jnp.float32,
        )

    def multiply(chunk):
        wigner_copy(chunk).wait()

        def pair(step, carry):
            first = chunk * chunk_orders + 2 * step
            place = pl.ds(pl.multiple_of(step * 2 * rows, 2 * rows), 2 * rows)
            for beam_order in range(wigner.shape[1]):
                lanes = pl.ds(beam_order * wigner.shape[2], wigner.shape[2])
                one = product(first, beam_order)
                two = product(first + 1, beam_order)
                for target, low in ((partial_own, 0), (partial_out, own_rows)):
                    target[chunk, :, place, lanes] = jnp.concatenate(
                        [
                            one[low : low + own_rows].reshape(count, rows, -1),
                            two[low : low + own_rows].reshape(count, rows, -1),
                        ],
                        axis=1,
                    )
            return carry

        lax.fori_loop(0, chunk_orders // 2, pair, 0, unroll=True)

    def pair_copy(chunk):
        return pltpu.make_async_remote_copy(
            src_ref=partial_out.at[chunk],
            dst_ref=partial_in.at[chunk],
            send_sem=pair_send.at[chunk],
            recv_sem=pair_recv.at[chunk],
            device_id=(partner, me),
            device_id_type=MESH,
        )

    def spec_copy(chunk, target, source):
        return pltpu.make_async_remote_copy(
            src_ref=spectra_out.at[chunk, target],
            dst_ref=spectra_in.at[source, chunk],
            send_sem=spec_send.at[chunk],
            recv_sem=spec_recv.at[chunk],
            device_id=(det, target),
            device_id_type=MESH,
        )

    def spread(chunk):
        pair_copy(chunk).wait_recv()
        total = (partial_own[chunk] + partial_in[chunk]).astype(jnp.bfloat16)
        spectra_out[chunk] = total

        for step in range(count - 1):
            spec_copy(chunk, lax.rem(me + 1 + (step + PLANE - 1) % (count - 1), count), me).start()
        spectra_in[me, chunk] = spectra_out[chunk, me]

    for chunk in range(CHUNKS):
        multiply(chunk)
        if chunk == 0:
            pl.semaphore_wait(barrier, count)
            info[det, near, plane] = info_ref[...]
            for step in range(1, planes):
                info_copy(step).start()
        pair_copy(chunk).start()
        if chunk > 0:
            spread(chunk - 1)
        if chunk == CHUNKS // 2:
            await_bytes(info.at[det, near, pl.ds(0, planes - 1)], info_recv)
            for step in range(1, PLANE):
                column_copy(step).start()
    spread(CHUNKS - 1)

    await_bytes(info.at[det, pl.ds(0, PLANE - 1)], column_recv)
    share_copy = pltpu.make_async_remote_copy(
        src_ref=info.at[det],
        dst_ref=info.at[det],
        send_sem=share_send,
        recv_sem=share_recv,
        device_id=(partner, me),
        device_id_type=MESH,
    )
    share_copy.start()

    shape = (2 * TILE, TILE)
    place = lax.broadcasted_iota(jnp.int32, shape, 0)
    place = jnp.where(place < 3 * TILE // 2, place, place - 2 * TILE)
    lag = place - lax.broadcasted_iota(jnp.int32, shape, 1)
    reach = taps_ref.shape[0] // 2

    def add_tap(place, total):
        return jnp.where(lag == place - reach, taps_ref[place], total)

    band_values = lax.fori_loop(0, taps_ref.shape[0], add_tap, jnp.zeros(shape, jnp.float32))
    band_high, band_low = split_parts(band_values)
    band[:, :TILE] = band_high
    band[:, TILE:] = band_low

    pltpu.make_async_remote_copy(
        src_ref=info.at[partner],
        dst_ref=info.at[partner],
        send_sem=share_send,
        recv_sem=share_recv,
        device_id=(partner, me),
        device_id_type=MESH,
    ).wait_recv()

    lane = lax.broadcasted_iota(jnp.int32, (blocks, TILE), 1)
    each = TILE // groups
    group = lane // each
    items = cube.shape[0] // groups
    half_rows = blocks // 2

    def prepare(n, carry):
        wanted = info[0, n % PLANE, n // PLANE, 2 * half_rows : 2 * half_rows + 1, :]
        ids = jnp.broadcast_to(wanted, (TILE, TILE)).T
        for part in range(cube.shape[0] // TILE):
            places = lax.broadcasted_iota(jnp.int32, (TILE, TILE), 1) + part * TILE
            picks[n, :, part * TILE : (part + 1) * TILE] = jnp.where(
                ids == places.astype(jnp.float32), 1.0, 0.0
            ).astype(jnp.bfloat16)
        offset = jnp.concatenate([info[0, n % PLANE, n // PLANE, :half_rows], info[1, n % PLANE, n // PLANE, :half_rows]], axis=0)
        fraction = jnp.concatenate(
            [info[0, n % PLANE, n // PLANE, half_rows : 2 * half_rows], info[1, n % PLANE, n // PLANE, half_rows : 2 * half_rows]],
            axis=0,
        )
        for b in range(groups):
            spot = b * each + lane % each
            start = jnp.take_along_axis(offset, spot, axis=1, mode="promise_in_bounds")
            f = jnp.take_along_axis(fraction, spot, axis=1, mode="promise_in_bounds")
            shifts[n, b] = start.astype(jnp.int32) + group
            weights[n, b] = (
                jnp.where(group == 0, -1.0 / 6.0, f + 1.0)
                * jnp.where(group == 1, 0.5, f)
                * jnp.where(group == 2, -0.5, f - 1.0)
                * jnp.where(group == 3, 1.0 / 6.0, f - 2.0)
            )
        return carry

    lax.fori_loop(0, intervals, prepare, 0)

    table_copy.wait()
    chunk_rows = spectra_in.shape[2]
    for chunk in range(CHUNKS):
        await_bytes(spectra_in.at[pl.ds(0, count - 1), chunk], spec_recv.at[chunk])
        spectra = spectra_in[:, chunk].reshape(count * chunk_rows, items)
        for b in range(groups):
            columns = pl.ds(b * per * TILE, per * TILE)
            total = sum(
                lax.dot_general(
                    spectra,
                    table[part, chunk, :, columns],
                    (((0,), (0,)), ((), ())),
                    preferred_element_type=jnp.float32,
                )
                for part in range(2)
            )
            place = pl.ds(b * items, items)
            if chunk > 0:
                total = total + field[place]
            if chunk < CHUNKS - 1:
                field[place] = total
            else:
                cube[place] = total.astype(jnp.bfloat16)

    margin = 8
    for d in range(per):
        series[d, :margin] = jnp.zeros((margin, TILE), jnp.float32)
        series[d, margin + intervals * blocks :] = jnp.zeros((margin, TILE), jnp.float32)

    batch = tiles.shape[0] // TILE

    def sample(first, place_in_batch):
        n = first + place_in_batch
        near = pl.multiple_of(place_in_batch * TILE, TILE)
        for d in range(per):
            terms = [
                jnp.take_along_axis(
                    tiles[pl.ds(near + b * blocks, blocks), d * TILE : (d + 1) * TILE],
                    shifts[n, b],
                    axis=1,
                    mode="promise_in_bounds",
                )
                * weights[n, b]
                for b in range(groups)
            ]
            total = jnp.zeros((blocks, TILE), jnp.float32)
            for k in range(groups):
                moved = terms[(groups - 1 - k) % groups]
                for t in range(groups - 1):
                    moved = jnp.where(group == t, terms[(t - k) % groups], moved)
                if k:
                    moved = pltpu.roll(moved, TILE - k * each, 1)
                total = total + moved
            place = pl.ds(pl.multiple_of(margin + n * blocks, 8), blocks)
            series[d, place] = total.astype(jnp.bfloat16).astype(jnp.float32)

    def out_copy(target, source):
        return pltpu.make_async_remote_copy(
            src_ref=signal_out.at[target],
            dst_ref=signal_in.at[source],
            send_sem=out_send,
            recv_sem=out_recv,
            device_id=(det, target),
            device_id_type=MESH,
        )

    def smooth(targets):
        windows = []
        for n in targets:
            for d in range(per):
                rows_near = series[d, pl.ds(pl.multiple_of(n * blocks, 8), blocks + 2 * margin)]
                before, here, after = (
                    rows_near[margin + s : margin + s + blocks] for s in (-1, 0, 1)
                )
                sides = jnp.where(lane < TILE // 2, after, before)
                windows.append(jnp.concatenate([here, sides], axis=1))
        window = jnp.concatenate(windows, axis=0).astype(jnp.bfloat16)
        both = jnp.dot(window, band[...], preferred_element_type=jnp.float32)
        smoothed = (both[:, :TILE] + both[:, TILE:]).astype(jnp.bfloat16)
        smoothed = smoothed.reshape(len(targets), per, blocks, TILE)
        for place, n in enumerate(targets):
            signal_out[n] = smoothed[place]

    def send(target):
        @pl.when(target != me)
        def _():
            out_copy(target, me).start()

    batches = intervals // batch
    origin = (me // batch + 1) * batch

    def one_batch(turn, carry):
        first = lax.rem(origin + turn * batch, intervals)
        chosen = picks[pl.ds(first, batch)].reshape(batch * TILE, -1)
        tiles[...] = jnp.dot(chosen, cube[...], preferred_element_type=jnp.float32)
        for step in range(batch):
            sample(first, step)
        targets = [lax.rem(first + intervals - 1 + step, intervals) for step in range(batch)]

        @pl.when(turn == 0)
        def _():
            smooth(targets[2:])

        @pl.when(turn > 0)
        def _():
            smooth(targets)
            for target in targets[:2]:
                send(target)

        for target in targets[2:]:
            send(target)
        return carry

    lax.fori_loop(0, batches, one_batch, 0)
    targets = [lax.rem(origin + intervals - 1 + step, intervals) for step in range(2)]
    smooth(targets)
    for target in targets:
        send(target)

    signal_in[me] = signal_out[me]
    await_bytes(signal_in.at[pl.ds(0, count - 1)], out_recv)
    wide[...] = signal_in[...].astype(jnp.float32).reshape(wide.shape)
    rows_out = out_ref.shape[0]
    for block in range(blocks):
        parts = [
            wide[pl.ds(first * blocks + block, 8, stride=blocks), :]
            for first in range(0, rows_out, 8)
        ]
        out_ref[:, block * TILE : (block + 1) * TILE] = jnp.concatenate(parts, axis=0).astype(
            out_ref.dtype
        )

    await_bytes(info.at[det, near, pl.ds(0, planes - 1)], info_send)
    await_bytes(info.at[det, pl.ds(0, PLANE - 1)], column_send)
    await_bytes(signal_out.at[pl.ds(0, count - 1)], out_send)
    for chunk in range(CHUNKS):
        await_bytes(spectra_out.at[chunk, pl.ds(0, count - 1)], spec_send.at[chunk])
    for chunk in range(CHUNKS):
        pair_copy(chunk).wait_send()
    share_copy.wait_send()


def local_fused(wigner, alm, beam, crossing, offsets, fraction, taps):
    det_count = lax.axis_size("det")
    count = lax.axis_size("ord")
    orders, beams, lats, depth = wigner.shape
    dets = beam.shape[0]
    per = dets // det_count // count
    orders_total = orders * count
    longitudes = 2 * orders_total
    groups = longitudes // TILE
    items = beams * lats
    tiles = items * groups
    intervals = count
    blocks = offsets.shape[1] // TILE
    chunk_rows = orders // CHUNKS * per * 2

    table = fourier_tables(orders_total, per).reshape(
        2, count, CHUNKS, chunk_rows, longitudes * per
    )
    table = jnp.asarray(
        np.swapaxes(table, 1, 2).reshape(2, CHUNKS, count * chunk_rows, longitudes * per)
    )

    f32, bf16 = jnp.float32, jnp.bfloat16
    dma = pltpu.SemaphoreType.DMA
    vmem = pl.BlockSpec(memory_space=pltpu.VMEM)
    anywhere = pl.BlockSpec(memory_space=pl.ANY)
    partial = pltpu.VMEM((CHUNKS, count, chunk_rows, items), f32)
    outgoing = pltpu.VMEM((CHUNKS, count, chunk_rows, items), bf16)
    arriving = pltpu.VMEM((count, CHUNKS, chunk_rows, items), bf16)
    result = pl.pallas_call(
        functools.partial(kernel, count, per, intervals, groups),
        out_shape=jax.ShapeDtypeStruct((count * per, blocks * TILE), bf16),
        in_specs=[
            anywhere, anywhere, anywhere, anywhere, vmem, vmem, vmem,
            pl.BlockSpec(memory_space=pltpu.SMEM),
        ],
        out_specs=vmem,
        scratch_shapes=[
            pltpu.VMEM((dets, beams, depth), bf16),
            pltpu.VMEM((orders, 2, depth), bf16),
            pltpu.VMEM((beams, dets * 2, depth), bf16),
            pltpu.VMEM((orders, 16, depth), bf16),
            pltpu.VMEM(wigner.shape, bf16),
            pltpu.VMEM(table.shape, bf16),
            partial, partial, partial, outgoing, arriving,
            pltpu.VMEM((INFO_ROWS, TILE), f32),
            pltpu.VMEM((2, PLANE, count // PLANE, INFO_ROWS, TILE), f32),
            pltpu.VMEM((intervals, TILE, tiles), bf16),
            pltpu.VMEM((intervals, groups, blocks, TILE), jnp.int32),
            pltpu.VMEM((intervals, groups, blocks, TILE), f32),
            pltpu.VMEM((2 * TILE, 2 * TILE), bf16),
            pltpu.VMEM((tiles, per * TILE), f32),
            pltpu.VMEM((tiles, per * TILE), bf16),
            pltpu.VMEM((BATCH * TILE, per * TILE), f32),
            pltpu.VMEM((per, intervals * blocks + 16, TILE), f32),
            pltpu.VMEM((count, per, blocks, TILE), bf16),
            pltpu.VMEM((count, per, blocks, TILE), bf16),
            pltpu.VMEM((count * per * blocks, TILE), f32),
            dma((2,)), dma((CHUNKS,)), dma, dma, dma, dma, dma, dma, dma,
            dma((CHUNKS,)), dma((CHUNKS,)), dma((CHUNKS,)), dma((CHUNKS,)),
            dma, dma,
        ],
        compiler_params=pltpu.CompilerParams(
            collective_id=0, has_side_effects=True, vmem_limit_bytes=56 * 2**20
        ),
    )(
        wigner,
        beam,
        alm,
        table,
        crossing,
        offsets.reshape(blocks, TILE),
        fraction.reshape(blocks, TILE),
        taps,
    )
    return result.astype(f32)


def with_halo(cells, sides, width):
    for axis, dim in sides:
        count = lax.axis_size(axis)
        ends = count - 1
        head = lax.slice_in_dim(cells, 0, width, axis=dim)
        tail = lax.slice_in_dim(cells, cells.shape[dim] - width, cells.shape[dim], axis=dim)
        cells = jnp.concatenate(
            [
                lax.ppermute(tail, axis, [(i, (i + 1) % count) for i in range(ends)]),
                cells,
                lax.ppermute(head, axis, [((i + 1) % count, i) for i in range(ends)]),
            ],
            axis=dim,
        )
    return cells


def lagrange_weights(position):
    shifted = position + 1.0
    minus_one = position - 1.0
    minus_two = position - 2.0
    return (
        -position * minus_one * minus_two / 6.0,
        shifted * minus_one * minus_two / 2.0,
        -shifted * position * minus_two / 2.0,
        shifted * position * minus_one / 6.0,
    )


def stencil_matrix(offset_part, fraction_part, width):
    columns = jnp.arange(width, dtype=jnp.int32)
    distance = columns[:, None] - offset_part[..., None, :]
    factors = lagrange_weights(fraction_part[..., None, :])
    matrix = jnp.zeros(distance.shape, jnp.float32)
    for place in range(4):
        matrix = matrix + jnp.where(distance == place, factors[place], 0.0)
    return matrix


def sky_beam(alm_part, beam_part):
    product = (
        beam_part.astype(jnp.float32)[:, None, :, None, :]
        * alm_part.astype(jnp.float32)[None, :, None, :, :]
    )
    return product.astype(jnp.bfloat16)


def local(wigner, alm, beam, crossing, offsets, fraction, taps):
    det_count = lax.axis_size("det")
    det_index = lax.axis_index("det")
    ord_count = lax.axis_size("ord")
    orders_local = wigner.shape[0]
    half_width = wigner.shape[3]
    det_local = beam.shape[0] // det_count
    alm_half = lax.dynamic_slice_in_dim(alm, det_index * half_width, half_width, 2)
    beam_half = lax.dynamic_slice_in_dim(beam, det_index * half_width, half_width, 2)
    spectra = lax.psum_scatter(
        jnp.einsum(
            "mkrl,jmkcl->jkrcm",
            wigner,
            sky_beam(alm_half, beam_half),
            preferred_element_type=jnp.float32,
        ),
        "det",
        scatter_dimension=0,
        tiled=True,
    )
    items_all = wigner.shape[1] * wigner.shape[2]
    outgoing = spectra.astype(jnp.bfloat16).reshape(det_local, items_all, 2 * orders_local)
    arrived = lax.all_to_all(outgoing, "ord", split_axis=1, concat_axis=2, tiled=True)
    items_local = items_all // ord_count
    spectrum = arrived.reshape(det_local, items_local, ord_count, 2, orders_local).astype(
        jnp.float32
    )
    orders_total = ord_count * orders_local
    longitudes = 2 * orders_total
    block = math.gcd(512, longitudes)
    order_ids = (
        jnp.arange(ord_count, dtype=jnp.int32)[:, None] * orders_local
        + jnp.arange(orders_local, dtype=jnp.int32)[None, :]
    )
    weight_row = (jnp.where(order_ids == 0, 1.0, 2.0) / math.sqrt(longitudes))[:, :, None]
    step_angle = 2.0 * math.pi / longitudes
    base_phase = (
        order_ids[:, :, None] * jnp.arange(block, dtype=jnp.int32)[None, None, :] % longitudes
    )
    base_angle = base_phase.astype(jnp.float32) * step_angle
    base_cos = jnp.cos(base_angle)
    base_sin = jnp.sin(base_angle)
    pieces = []
    for first in range(0, longitudes, block):
        shift_angle = (order_ids * first % longitudes).astype(jnp.float32)[:, :, None] * step_angle
        shift_cos = jnp.cos(shift_angle)
        shift_sin = jnp.sin(shift_angle)
        cos_block = base_cos * shift_cos - base_sin * shift_sin
        sin_block = base_sin * shift_cos + base_cos * shift_sin
        table = jnp.stack([weight_row * cos_block, -weight_row * sin_block], axis=1)
        pieces.append(
            jnp.einsum("jincs,ncsp->ijp", spectrum, table, precision=lax.Precision.HIGHEST)
        )
    cube = jnp.concatenate(pieces, axis=2).astype(jnp.bfloat16)
    tile_width = TILE
    blocks_per_item = longitudes // tile_width
    tiles = cube.reshape(items_local, det_local, blocks_per_item, tile_width).transpose(0, 2, 1, 3)
    tiles = tiles.reshape(items_local * blocks_per_item, det_local, tile_width)
    tiles_local = tiles.shape[0]
    wanted = crossing[0]
    crossings = wanted.shape[0]
    capacity = max(2, 2 * crossings // ord_count)
    holder = wanted // tiles_local
    local_ids = wanted % tiles_local
    order_index = jnp.arange(crossings, dtype=jnp.int32)
    earlier = (holder[:, None] == holder[None, :]) & (order_index[None, :] < order_index[:, None])
    slot_ids = jnp.sum(earlier.astype(jnp.int32), axis=1)
    flat_slot = holder * capacity + slot_ids
    chosen = flat_slot[:, None] == jnp.arange(ord_count * capacity, dtype=jnp.int32)[None, :]
    requests = (jnp.sum(jnp.where(chosen, local_ids[:, None] + 1, 0), axis=0) - 1).reshape(
        ord_count, capacity
    )
    offset_rows = offsets[0].reshape(crossings, -1)
    fraction_rows = fraction[0].reshape(crossings, -1)
    samples_each = offset_rows.shape[1]
    slot_crossing = jnp.sum(jnp.where(chosen, order_index[:, None], 0), axis=0)
    occupied = jnp.any(chosen, axis=0)
    slot_offsets = jnp.where(occupied[:, None], offset_rows[slot_crossing], 0)
    slot_offsets = slot_offsets.reshape(ord_count, capacity, samples_each)
    slot_fractions = jnp.where(occupied[:, None], fraction_rows[slot_crossing], 0.0)
    slot_fractions = slot_fractions.reshape(ord_count, capacity, samples_each)
    asked = lax.all_to_all(requests, "ord", split_axis=0, concat_axis=0, tiled=True)
    asked_offsets = lax.all_to_all(slot_offsets, "ord", split_axis=0, concat_axis=0, tiled=True)
    asked_fractions = lax.all_to_all(slot_fractions, "ord", split_axis=0, concat_axis=0, tiled=True)
    stencil = stencil_matrix(asked_offsets, asked_fractions, tile_width)
    present = asked >= 0
    picked = tiles[jnp.maximum(asked, 0)]
    result = jnp.einsum(
        "rnjo,rnos->rnjs",
        jnp.where(present[..., None, None], picked, jnp.zeros((), jnp.bfloat16)).astype(
            jnp.float32
        ),
        stencil,
        precision=lax.Precision.HIGHEST,
    )
    received = lax.all_to_all(
        result.astype(jnp.bfloat16), "ord", split_axis=0, concat_axis=0, tiled=True
    )
    samples = jnp.transpose(received[holder, slot_ids], (1, 0, 2)).reshape(det_local, -1)
    reach = taps.shape[0] // 2
    extended = with_halo(samples, (("ord", 1),), reach)
    total_time = samples.shape[1]
    padded = jnp.concatenate(
        [extended, jnp.zeros((det_local, 128 - 2 * reach), jnp.bfloat16)], axis=1
    )
    windows = jnp.concatenate(
        [
            padded[:, :total_time].reshape(det_local, -1, 128),
            padded[:, 128 : total_time + 128].reshape(det_local, -1, 128),
        ],
        axis=2,
    )
    lag_index = (
        jnp.arange(256, dtype=jnp.int32)[:, None] - jnp.arange(128, dtype=jnp.int32)[None, :]
    )
    inside = (lag_index >= 0) & (lag_index < taps.shape[0])
    banded = jnp.where(inside, taps[jnp.clip(lag_index, 0, taps.shape[0] - 1)], 0.0)
    smoothed = jnp.einsum(
        "jbu,uo->jbo", windows.astype(jnp.float32), banded, precision=lax.Precision.HIGHEST
    )
    return smoothed.reshape(det_local, total_time)


def splits_detectors(mesh, wigner, beam, offsets):
    count = mesh.shape["ord"]
    return (
        mesh.shape["det"] == 2
        and beam.shape[0] == 4 * count
        and wigner.shape[0] == 4 * CHUNKS * count
        and 2 * wigner.shape[0] == 4 * TILE
        and wigner.shape[1:3] == (2, TILE)
        and offsets.shape == (count, 32 * TILE)
        and count % BATCH == 0
        and count % PLANE == 0
    )


def solution(mesh):
    def run(wigner, alm, beam, crossing, offsets, fraction, taps):
        fused = splits_detectors(mesh, wigner, beam, offsets)
        return jax.shard_map(
            local_fused if fused else local,
            mesh=mesh,
            in_specs=(
                P("ord", None, None, "det"),
                P("ord", None),
                P(),
                P("ord"),
                P("ord"),
                P("ord"),
                P(),
            ),
            out_specs=P("det", "ord"),
            check_vma=False,
        )(wigner, alm, beam, crossing, offsets, fraction, taps)

    return run
```

```python
import functools
import math

import jax
import jax.numpy as jnp
import numpy as np
from jax import lax
from jax.experimental import pallas as pl
from jax.experimental.pallas import tpu as pltpu
from jax.sharding import PartitionSpec as P

TILE = 128
CHUNKS = 4
PLANE = 4
BATCH = 4
INFO_ROWS = 40
MESH = pl.DeviceIdType.MESH


def split_parts(values):
    high = values.astype(jnp.bfloat16)
    return high, (values - high.astype(jnp.float32)).astype(jnp.bfloat16)


def fourier_tables(orders_total, per):
    longitudes = 2 * orders_total
    order = np.arange(orders_total, dtype=np.int64)
    phase = (order[:, None] * np.arange(longitudes)[None, :]) % longitudes
    angle = phase * (2.0 * math.pi / longitudes)
    weight = np.where(order == 0, 1.0, 2.0)[:, None] / math.sqrt(longitudes)
    parts = np.stack([weight * np.cos(angle), -weight * np.sin(angle)], axis=1)
    parts = parts.reshape(orders_total, 2, longitudes // TILE, TILE)
    table = np.zeros((orders_total, per, 2, longitudes // TILE, per, TILE), np.float32)
    for det in range(per):
        table[:, det, :, :, det, :] = parts
    table = table.reshape(orders_total * per * 2, longitudes * per)
    high = table.astype(jnp.bfloat16)
    low = (table - high.astype(np.float32)).astype(jnp.bfloat16)
    return np.stack([high, low])


def kernel(
    count, per, intervals, tiles_per_item,
    wigner_hbm, beam_hbm, alm_hbm, table_hbm, crossing_ref, offsets_ref, fraction_ref, taps_ref,
    out_ref,
    beam_in, alm_in, beam_ref, alm_ref,
    wigner, table, partial_own, partial_out, partial_in, spectra_out, spectra_in,
    info_ref, info, picks, shifts, weights, band, field, cube, tiles, series,
    signal_out,
    small_sem, wigner_sem, table_sem, info_send, info_recv, column_send, column_recv, share_send, share_recv,
    pair_send, pair_recv, spec_send, spec_recv, out_send, out_recv,
):
    det = lax.axis_index("det")
    me = lax.axis_index("ord")
    partner = 1 - det
    orders = wigner.shape[0]
    chunk_orders = orders // CHUNKS
    blocks = shifts.shape[2]
    groups = tiles_per_item

    def wigner_copy(chunk):
        part = pl.ds(chunk * chunk_orders, chunk_orders)
        return pltpu.make_async_copy(wigner_hbm.at[part], wigner.at[part], wigner_sem.at[chunk])

    depth = beam_in.shape[2]
    near_depth = pl.ds(pl.multiple_of(det * depth, TILE), depth)
    beam_copy = pltpu.make_async_copy(beam_hbm.at[:, :, near_depth], beam_in, small_sem.at[0])
    alm_copy = pltpu.make_async_copy(alm_hbm.at[:, :, near_depth], alm_in, small_sem.at[1])
    beam_copy.start()
    alm_copy.start()
    for chunk in range(CHUNKS):
        wigner_copy(chunk).start()
    table_copy = pltpu.make_async_copy(table_hbm, table, table_sem)
    table_copy.start()

    barrier = pltpu.get_barrier_semaphore()

    def greet(step, carry):
        peer = lax.rem(me + step, count)
        pl.semaphore_signal(barrier, inc=1, device_id=(det, peer), device_id_type=MESH)
        return carry

    lax.fori_loop(1, count, greet, 0)
    pl.semaphore_signal(barrier, inc=1, device_id=(partner, me), device_id_type=MESH)

    def select_rows(source, wanted_column):
        chosen = jnp.where(
            wanted_column == lax.broadcasted_iota(jnp.int32, wanted_column.shape, 1), 1.0, 0.0
        ).astype(jnp.bfloat16)
        return jnp.dot(chosen, source, preferred_element_type=jnp.float32).astype(jnp.bfloat16)

    beams = wigner.shape[1]
    beam_copy.wait()
    beam_rows_all = beam_ref.shape[1]
    beam_source = beam_in[...].reshape(-1, depth)
    row = lax.broadcasted_iota(jnp.int32, (beam_rows_all, beam_source.shape[0]), 0)
    half_rows = beam_rows_all // 2
    side = lax.rem(row // half_rows + det, 2)
    beam_column = (side * (half_rows // 2) + row % half_rows // 2) * beams
    for beam_order in range(beams):
        beam_ref[beam_order] = select_rows(beam_source, beam_column + beam_order)
    alm_copy.wait()
    repeat = alm_ref.shape[1]
    alm_source = alm_in[...].reshape(-1, depth)
    row = lax.broadcasted_iota(jnp.int32, (orders * repeat, alm_source.shape[0]), 0)
    alm_ref[...] = select_rows(alm_source, row // repeat * 2 + row % 2).reshape(
        alm_ref.shape
    )

    half_blocks = blocks // 2
    near_blocks = pl.ds(pl.multiple_of(det * half_blocks, 8), half_blocks)
    info_ref[:half_blocks] = offsets_ref[near_blocks].astype(jnp.float32)
    info_ref[half_blocks : 2 * half_blocks] = fraction_ref[near_blocks]
    ids = jnp.broadcast_to(crossing_ref[...], (8, TILE))
    ids = ids % groups * (cube.shape[0] // groups) + ids // groups
    lanes_row = lax.broadcasted_iota(jnp.int32, (8, TILE), 1)
    info_ref[2 * half_blocks :] = jnp.take_along_axis(
        ids.astype(jnp.float32),
        lanes_row % blocks * groups + lanes_row // blocks,
        axis=1,
        mode="promise_in_bounds",
    )

    planes = count // PLANE
    near, plane = lax.rem(me, PLANE), me // PLANE

    def info_copy(step):
        return pltpu.make_async_remote_copy(
            src_ref=info_ref,
            dst_ref=info.at[det, near, plane],
            send_sem=info_send,
            recv_sem=info_recv,
            device_id=(det, lax.rem(me + step * PLANE, count)),
            device_id_type=MESH,
        )

    def column_copy(step):
        return pltpu.make_async_remote_copy(
            src_ref=info.at[det, near],
            dst_ref=info.at[det, near],
            send_sem=column_send,
            recv_sem=column_recv,
            device_id=(det, plane * PLANE + lax.rem(near + step, PLANE)),
            device_id_type=MESH,
        )

    def await_bytes(block, semaphore):
        pltpu.make_async_copy(block, block, semaphore).wait()

    rows = per * 2
    own_rows = count * rows

    def product(order, beam_order):
        alm_rows = alm_ref[order]
        beam_rows = beam_ref[beam_order]
        sky = beam_rows.reshape(-1, alm_rows.shape[0], depth) * alm_rows[None]
        return lax.dot_general(
            sky.reshape(-1, depth),
            wigner[order, beam_order],
            (((1,), (1,)), ((), ())),
            preferred_element_type=jnp.float32,
        )

    def multiply(chunk):
        wigner_copy(chunk).wait()

        def pair(step):
            first = chunk * chunk_orders + 2 * step
            place = pl.ds(step * 2 * rows, 2 * rows)
            for beam_order in range(wigner.shape[1]):
                lanes = pl.ds(beam_order * wigner.shape[2], wigner.shape[2])
                one = product(first, beam_order)
                two = product(first + 1, beam_order)
                for target, low in ((partial_own, 0), (partial_out, own_rows)):
                    target[chunk, :, place, lanes] = jnp.concatenate(
                        [
                            one[low : low + own_rows].reshape(count, rows, -1),
                            two[low : low + own_rows].reshape(count, rows, -1),
                        ],
                        axis=1,
                    )

        for step in range(chunk_orders // 2):
            pair(step)
            if step == 0 and chunk > 0:
                spread(chunk - 1)

    def pair_copy(chunk):
        return pltpu.make_async_remote_copy(
            src_ref=partial_out.at[chunk],
            dst_ref=partial_in.at[chunk],
            send_sem=pair_send.at[chunk],
            recv_sem=pair_recv.at[chunk],
            device_id=(partner, me),
            device_id_type=MESH,
        )

    def spec_copy(chunk, target, source):
        return pltpu.make_async_remote_copy(
            src_ref=spectra_out.at[chunk, target],
            dst_ref=spectra_in.at[source, chunk],
            send_sem=spec_send.at[chunk],
            recv_sem=spec_recv.at[chunk],
            device_id=(det, target),
            device_id_type=MESH,
        )

    def spread(chunk):
        pair_copy(chunk).wait_recv()
        total = (partial_own[chunk] + partial_in[chunk]).astype(jnp.bfloat16)
        spectra_out[chunk] = total

        for step in range(count - 1):
            spec_copy(chunk, lax.rem(me + 1 + (step + PLANE - 1) % (count - 1), count), me).start()
        spectra_in[me, chunk] = spectra_out[chunk, me]

    for chunk in range(CHUNKS):
        multiply(chunk)
        if chunk == 0:
            pl.semaphore_wait(barrier, count)
            info[det, near, plane] = info_ref[...]
            for step in range(1, planes):
                info_copy(step).start()
        pair_copy(chunk).start()
        if chunk == CHUNKS // 2:
            await_bytes(info.at[det, near, pl.ds(0, planes - 1)], info_recv)
            for step in range(1, PLANE):
                column_copy(step).start()
    spread(CHUNKS - 1)

    await_bytes(info.at[det, pl.ds(0, PLANE - 1)], column_recv)
    share_copy = pltpu.make_async_remote_copy(
        src_ref=info.at[det],
        dst_ref=info.at[det],
        send_sem=share_send,
        recv_sem=share_recv,
        device_id=(partner, me),
        device_id_type=MESH,
    )
    share_copy.start()

    shape = (2 * TILE, TILE)
    place = lax.broadcasted_iota(jnp.int32, shape, 0)
    place = jnp.where(place < 3 * TILE // 2, place, place - 2 * TILE)
    lag = place - lax.broadcasted_iota(jnp.int32, shape, 1)
    reach = taps_ref.shape[0] // 2

    def add_tap(place, total):
        return jnp.where(lag == place - reach, taps_ref[place], total)

    band_values = lax.fori_loop(0, taps_ref.shape[0], add_tap, jnp.zeros(shape, jnp.float32))
    band_high, band_low = split_parts(band_values)
    band[:, :TILE] = band_high
    band[:, TILE:] = band_low

    pltpu.make_async_remote_copy(
        src_ref=info.at[partner],
        dst_ref=info.at[partner],
        send_sem=share_send,
        recv_sem=share_recv,
        device_id=(partner, me),
        device_id_type=MESH,
    ).wait_recv()

    lane = lax.broadcasted_iota(jnp.int32, (blocks, TILE), 1)
    each = TILE // groups
    group = lane // each
    items = cube.shape[0] // groups
    half_rows = blocks // 2

    places = lax.broadcasted_iota(jnp.int32, (TILE, TILE), 1).astype(jnp.float32)

    def prepare(n, carry):
        wanted = info[0, n % PLANE, n // PLANE, 2 * half_rows : 2 * half_rows + 1, :]
        ids = jnp.broadcast_to(wanted, (TILE, TILE)).T
        for part in range(cube.shape[0] // TILE):
            picks[n, :, part * TILE : (part + 1) * TILE] = jnp.where(
                ids - part * TILE == places, 1.0, 0.0
            ).astype(jnp.bfloat16)
        offset = jnp.concatenate([info[0, n % PLANE, n // PLANE, :half_rows], info[1, n % PLANE, n // PLANE, :half_rows]], axis=0)
        fraction = jnp.concatenate(
            [info[0, n % PLANE, n // PLANE, half_rows : 2 * half_rows], info[1, n % PLANE, n // PLANE, half_rows : 2 * half_rows]],
            axis=0,
        )
        for b in range(groups):
            spot = b * each + lane % each
            start = jnp.take_along_axis(offset, spot, axis=1, mode="promise_in_bounds")
            f = jnp.take_along_axis(fraction, spot, axis=1, mode="promise_in_bounds")
            shifts[n, b] = start.astype(jnp.int32) + group
            weights[n, b] = (
                jnp.where(group == 0, -1.0 / 6.0, f + 1.0)
                * jnp.where(group == 1, 0.5, f)
                * jnp.where(group == 2, -0.5, f - 1.0)
                * jnp.where(group == 3, 1.0 / 6.0, f - 2.0)
            )
        return carry

    lax.fori_loop(0, intervals, prepare, 0, unroll=2)

    table_copy.wait()
    chunk_rows = spectra_in.shape[2]
    for chunk in range(CHUNKS):
        await_bytes(spectra_in.at[pl.ds(0, count - 1), chunk], spec_recv.at[chunk])
        spectra = spectra_in[:, chunk].reshape(count * chunk_rows, items)
        turned = spectra.T
        for b in range(groups):
            columns = pl.ds(b * per * TILE, per * TILE)
            total = sum(
                jnp.dot(
                    turned, table[part, chunk, :, columns], preferred_element_type=jnp.float32
                )
                for part in range(2)
            )
            place = pl.ds(b * items, items)
            if chunk > 0:
                total = total + field[place]
            if chunk < CHUNKS - 1:
                field[place] = total
            else:
                cube[place] = total.astype(jnp.bfloat16)

    margin = 8
    for d in range(per):
        series[d, :margin] = jnp.zeros((margin, TILE), jnp.float32)
        series[d, margin + intervals * blocks :] = jnp.zeros((margin, TILE), jnp.float32)

    batch = tiles.shape[0] // TILE

    def sample(first, place_in_batch):
        n = first + place_in_batch
        near = pl.multiple_of(place_in_batch * TILE, TILE)
        for d in range(per):
            terms = [
                jnp.take_along_axis(
                    tiles[pl.ds(near + b * blocks, blocks), d * TILE : (d + 1) * TILE],
                    shifts[n, b],
                    axis=1,
                    mode="promise_in_bounds",
                )
                * weights[n, b]
                for b in range(groups)
            ]
            total = jnp.zeros((blocks, TILE), jnp.float32)
            for k in range(groups):
                moved = terms[(groups - 1 - k) % groups]
                for t in range(groups - 1):
                    moved = jnp.where(group == t, terms[(t - k) % groups], moved)
                if k:
                    moved = pltpu.roll(moved, TILE - k * each, 1)
                total = total + moved
            place = pl.ds(pl.multiple_of(margin + n * blocks, 8), blocks)
            series[d, place] = total.astype(jnp.bfloat16).astype(jnp.float32)

    def out_copy(target, source):
        return pltpu.make_async_remote_copy(
            src_ref=signal_out.at[target],
            dst_ref=out_ref.at[source],
            send_sem=out_send,
            recv_sem=out_recv,
            device_id=(det, target),
            device_id_type=MESH,
        )

    def smooth(targets):
        windows = []
        for n in targets:
            for d in range(per):
                rows_near = series[d, pl.ds(pl.multiple_of(n * blocks, 8), blocks + 2 * margin)]
                before, here, after = (
                    rows_near[margin + s : margin + s + blocks] for s in (-1, 0, 1)
                )
                sides = jnp.where(lane < TILE // 2, after, before)
                windows.append(jnp.concatenate([here, sides], axis=1))
        window = jnp.concatenate(windows, axis=0).astype(jnp.bfloat16)
        both = jnp.dot(window, band[...], preferred_element_type=jnp.float32)
        smoothed = (both[:, :TILE] + both[:, TILE:]).astype(jnp.bfloat16)
        smoothed = smoothed.reshape(len(targets), per, blocks, TILE)
        for place, n in enumerate(targets):
            signal_out[n] = smoothed[place]

    def send(target):
        @pl.when(target != me)
        def _():
            out_copy(target, me).start()

    batches = intervals // batch
    origin = (me // batch + 1) * batch

    def one_batch(turn, carry):
        first = lax.rem(origin + turn * batch, intervals)
        chosen = picks[pl.ds(first, batch)].reshape(batch * TILE, -1)
        tiles[...] = jnp.dot(chosen, cube[...], preferred_element_type=jnp.float32)
        for step in range(batch):
            sample(first, step)
        targets = [lax.rem(first + intervals - 1 + step, intervals) for step in range(batch)]

        @pl.when(turn == 0)
        def _():
            smooth(targets[2:])

        @pl.when(turn > 0)
        def _():
            smooth(targets)
            for target in targets[:2]:
                send(target)

        for target in targets[2:]:
            send(target)
        return carry

    lax.fori_loop(0, batches, one_batch, 0)
    targets = [lax.rem(origin + intervals - 1 + step, intervals) for step in range(2)]
    smooth(targets)
    for target in targets:
        send(target)

    out_ref[me] = signal_out[me]
    await_bytes(out_ref.at[pl.ds(0, count - 1)], out_recv)
    await_bytes(info.at[det, near, pl.ds(0, planes - 1)], info_send)
    await_bytes(info.at[det, pl.ds(0, PLANE - 1)], column_send)
    await_bytes(signal_out.at[pl.ds(0, count - 1)], out_send)
    for chunk in range(CHUNKS):
        await_bytes(spectra_out.at[chunk, pl.ds(0, count - 1)], spec_send.at[chunk])
    for chunk in range(CHUNKS):
        pair_copy(chunk).wait_send()
    share_copy.wait_send()


def lay_out(signal_ref, out_ref, wide):
    rows, blocks = out_ref.shape[0], wide.shape[0] // out_ref.shape[0]
    wide[...] = signal_ref[...].astype(jnp.float32).reshape(wide.shape)
    for block in range(blocks):
        out_ref[:, block * TILE : (block + 1) * TILE] = wide[
            pl.ds(block, rows, stride=blocks), :
        ]


def local_fused(wigner, alm, beam, crossing, offsets, fraction, taps):
    det_count = lax.axis_size("det")
    count = lax.axis_size("ord")
    orders, beams, lats, depth = wigner.shape
    dets = beam.shape[0]
    per = dets // det_count // count
    orders_total = orders * count
    longitudes = 2 * orders_total
    groups = longitudes // TILE
    items = beams * lats
    tiles = items * groups
    intervals = count
    blocks = offsets.shape[1] // TILE
    chunk_rows = orders // CHUNKS * per * 2

    table = fourier_tables(orders_total, per).reshape(
        2, count, CHUNKS, chunk_rows, longitudes * per
    )
    table = jnp.asarray(
        np.swapaxes(table, 1, 2).reshape(2, CHUNKS, count * chunk_rows, longitudes * per)
    )

    f32, bf16 = jnp.float32, jnp.bfloat16
    dma = pltpu.SemaphoreType.DMA
    vmem = pl.BlockSpec(memory_space=pltpu.VMEM)
    anywhere = pl.BlockSpec(memory_space=pl.ANY)
    partial = pltpu.VMEM((CHUNKS, count, chunk_rows, items), f32)
    outgoing = pltpu.VMEM((CHUNKS, count, chunk_rows, items), bf16)
    arriving = pltpu.VMEM((count, CHUNKS, chunk_rows, items), bf16)
    result = pl.pallas_call(
        functools.partial(kernel, count, per, intervals, groups),
        out_shape=jax.ShapeDtypeStruct((count, per, blocks, TILE), bf16),
        in_specs=[
            anywhere, anywhere, anywhere, anywhere, vmem, vmem, vmem,
            pl.BlockSpec(memory_space=pltpu.SMEM),
        ],
        out_specs=vmem,
        scratch_shapes=[
            pltpu.VMEM((dets, beams, depth), bf16),
            pltpu.VMEM((orders, 2, depth), bf16),
            pltpu.VMEM((beams, dets * 2, depth), bf16),
            pltpu.VMEM((orders, 16, depth), bf16),
            pltpu.VMEM(wigner.shape, bf16),
            pltpu.VMEM(table.shape, bf16),
            partial, partial, partial, outgoing, arriving,
            pltpu.VMEM((INFO_ROWS, TILE), f32),
            pltpu.VMEM((2, PLANE, count // PLANE, INFO_ROWS, TILE), f32),
            pltpu.VMEM((intervals, TILE, tiles), bf16),
            pltpu.VMEM((intervals, groups, blocks, TILE), jnp.int32),
            pltpu.VMEM((intervals, groups, blocks, TILE), f32),
            pltpu.VMEM((2 * TILE, 2 * TILE), bf16),
            pltpu.VMEM((tiles, per * TILE), f32),
            pltpu.VMEM((tiles, per * TILE), bf16),
            pltpu.VMEM((BATCH * TILE, per * TILE), f32),
            pltpu.VMEM((per, intervals * blocks + 16, TILE), f32),
            pltpu.VMEM((count, per, blocks, TILE), bf16),
            dma((2,)), dma((CHUNKS,)), dma, dma, dma, dma, dma, dma, dma,
            dma((CHUNKS,)), dma((CHUNKS,)), dma((CHUNKS,)), dma((CHUNKS,)),
            dma, dma,
        ],
        compiler_params=pltpu.CompilerParams(
            collective_id=0, has_side_effects=True, vmem_limit_bytes=56 * 2**20
        ),
    )(
        wigner,
        beam,
        alm,
        table,
        crossing,
        offsets.reshape(blocks, TILE),
        fraction.reshape(blocks, TILE),
        taps,
    )
    return pl.pallas_call(
        lay_out,
        grid=(count * per // 8,),
        in_specs=[pl.BlockSpec((8 // per, per, blocks, TILE), lambda i: (i, 0, 0, 0))],
        out_specs=pl.BlockSpec((8, blocks * TILE), lambda i: (i, 0)),
        out_shape=jax.ShapeDtypeStruct((count * per, blocks * TILE), f32),
        scratch_shapes=[pltpu.VMEM((8 * blocks, TILE), f32)],
    )(result)


def with_halo(cells, sides, width):
    for axis, dim in sides:
        count = lax.axis_size(axis)
        ends = count - 1
        head = lax.slice_in_dim(cells, 0, width, axis=dim)
        tail = lax.slice_in_dim(cells, cells.shape[dim] - width, cells.shape[dim], axis=dim)
        cells = jnp.concatenate(
            [
                lax.ppermute(tail, axis, [(i, (i + 1) % count) for i in range(ends)]),
                cells,
                lax.ppermute(head, axis, [((i + 1) % count, i) for i in range(ends)]),
            ],
            axis=dim,
        )
    return cells


def lagrange_weights(position):
    shifted = position + 1.0
    minus_one = position - 1.0
    minus_two = position - 2.0
    return (
        -position * minus_one * minus_two / 6.0,
        shifted * minus_one * minus_two / 2.0,
        -shifted * position * minus_two / 2.0,
        shifted * position * minus_one / 6.0,
    )


def stencil_matrix(offset_part, fraction_part, width):
    columns = jnp.arange(width, dtype=jnp.int32)
    distance = columns[:, None] - offset_part[..., None, :]
    factors = lagrange_weights(fraction_part[..., None, :])
    matrix = jnp.zeros(distance.shape, jnp.float32)
    for place in range(4):
        matrix = matrix + jnp.where(distance == place, factors[place], 0.0)
    return matrix


def sky_beam(alm_part, beam_part):
    product = (
        beam_part.astype(jnp.float32)[:, None, :, None, :]
        * alm_part.astype(jnp.float32)[None, :, None, :, :]
    )
    return product.astype(jnp.bfloat16)


def local(wigner, alm, beam, crossing, offsets, fraction, taps):
    det_count = lax.axis_size("det")
    det_index = lax.axis_index("det")
    ord_count = lax.axis_size("ord")
    orders_local = wigner.shape[0]
    half_width = wigner.shape[3]
    det_local = beam.shape[0] // det_count
    alm_half = lax.dynamic_slice_in_dim(alm, det_index * half_width, half_width, 2)
    beam_half = lax.dynamic_slice_in_dim(beam, det_index * half_width, half_width, 2)
    spectra = lax.psum_scatter(
        jnp.einsum(
            "mkrl,jmkcl->jkrcm",
            wigner,
            sky_beam(alm_half, beam_half),
            preferred_element_type=jnp.float32,
        ),
        "det",
        scatter_dimension=0,
        tiled=True,
    )
    items_all = wigner.shape[1] * wigner.shape[2]
    outgoing = spectra.astype(jnp.bfloat16).reshape(det_local, items_all, 2 * orders_local)
    arrived = lax.all_to_all(outgoing, "ord", split_axis=1, concat_axis=2, tiled=True)
    items_local = items_all // ord_count
    spectrum = arrived.reshape(det_local, items_local, ord_count, 2, orders_local).astype(
        jnp.float32
    )
    orders_total = ord_count * orders_local
    longitudes = 2 * orders_total
    block = math.gcd(512, longitudes)
    order_ids = (
        jnp.arange(ord_count, dtype=jnp.int32)[:, None] * orders_local
        + jnp.arange(orders_local, dtype=jnp.int32)[None, :]
    )
    weight_row = (jnp.where(order_ids == 0, 1.0, 2.0) / math.sqrt(longitudes))[:, :, None]
    step_angle = 2.0 * math.pi / longitudes
    base_phase = (
        order_ids[:, :, None] * jnp.arange(block, dtype=jnp.int32)[None, None, :] % longitudes
    )
    base_angle = base_phase.astype(jnp.float32) * step_angle
    base_cos = jnp.cos(base_angle)
    base_sin = jnp.sin(base_angle)
    pieces = []
    for first in range(0, longitudes, block):
        shift_angle = (order_ids * first % longitudes).astype(jnp.float32)[:, :, None] * step_angle
        shift_cos = jnp.cos(shift_angle)
        shift_sin = jnp.sin(shift_angle)
        cos_block = base_cos * shift_cos - base_sin * shift_sin
        sin_block = base_sin * shift_cos + base_cos * shift_sin
        table = jnp.stack([weight_row * cos_block, -weight_row * sin_block], axis=1)
        pieces.append(
            jnp.einsum("jincs,ncsp->ijp", spectrum, table, precision=lax.Precision.HIGHEST)
        )
    cube = jnp.concatenate(pieces, axis=2).astype(jnp.bfloat16)
    tile_width = TILE
    blocks_per_item = longitudes // tile_width
    tiles = cube.reshape(items_local, det_local, blocks_per_item, tile_width).transpose(0, 2, 1, 3)
    tiles = tiles.reshape(items_local * blocks_per_item, det_local, tile_width)
    tiles_local = tiles.shape[0]
    wanted = crossing[0]
    crossings = wanted.shape[0]
    capacity = max(2, 2 * crossings // ord_count)
    holder = wanted // tiles_local
    local_ids = wanted % tiles_local
    order_index = jnp.arange(crossings, dtype=jnp.int32)
    earlier = (holder[:, None] == holder[None, :]) & (order_index[None, :] < order_index[:, None])
    slot_ids = jnp.sum(earlier.astype(jnp.int32), axis=1)
    flat_slot = holder * capacity + slot_ids
    chosen = flat_slot[:, None] == jnp.arange(ord_count * capacity, dtype=jnp.int32)[None, :]
    requests = (jnp.sum(jnp.where(chosen, local_ids[:, None] + 1, 0), axis=0) - 1).reshape(
        ord_count, capacity
    )
    offset_rows = offsets[0].reshape(crossings, -1)
    fraction_rows = fraction[0].reshape(crossings, -1)
    samples_each = offset_rows.shape[1]
    slot_crossing = jnp.sum(jnp.where(chosen, order_index[:, None], 0), axis=0)
    occupied = jnp.any(chosen, axis=0)
    slot_offsets = jnp.where(occupied[:, None], offset_rows[slot_crossing], 0)
    slot_offsets = slot_offsets.reshape(ord_count, capacity, samples_each)
    slot_fractions = jnp.where(occupied[:, None], fraction_rows[slot_crossing], 0.0)
    slot_fractions = slot_fractions.reshape(ord_count, capacity, samples_each)
    asked = lax.all_to_all(requests, "ord", split_axis=0, concat_axis=0, tiled=True)
    asked_offsets = lax.all_to_all(slot_offsets, "ord", split_axis=0, concat_axis=0, tiled=True)
    asked_fractions = lax.all_to_all(slot_fractions, "ord", split_axis=0, concat_axis=0, tiled=True)
    stencil = stencil_matrix(asked_offsets, asked_fractions, tile_width)
    present = asked >= 0
    picked = tiles[jnp.maximum(asked, 0)]
    result = jnp.einsum(
        "rnjo,rnos->rnjs",
        jnp.where(present[..., None, None], picked, jnp.zeros((), jnp.bfloat16)).astype(
            jnp.float32
        ),
        stencil,
        precision=lax.Precision.HIGHEST,
    )
    received = lax.all_to_all(
        result.astype(jnp.bfloat16), "ord", split_axis=0, concat_axis=0, tiled=True
    )
    samples = jnp.transpose(received[holder, slot_ids], (1, 0, 2)).reshape(det_local, -1)
    reach = taps.shape[0] // 2
    extended = with_halo(samples, (("ord", 1),), reach)
    total_time = samples.shape[1]
    padded = jnp.concatenate(
        [extended, jnp.zeros((det_local, 128 - 2 * reach), jnp.bfloat16)], axis=1
    )
    windows = jnp.concatenate(
        [
            padded[:, :total_time].reshape(det_local, -1, 128),
            padded[:, 128 : total_time + 128].reshape(det_local, -1, 128),
        ],
        axis=2,
    )
    lag_index = (
        jnp.arange(256, dtype=jnp.int32)[:, None] - jnp.arange(128, dtype=jnp.int32)[None, :]
    )
    inside = (lag_index >= 0) & (lag_index < taps.shape[0])
    banded = jnp.where(inside, taps[jnp.clip(lag_index, 0, taps.shape[0] - 1)], 0.0)
    smoothed = jnp.einsum(
        "jbu,uo->jbo", windows.astype(jnp.float32), banded, precision=lax.Precision.HIGHEST
    )
    return smoothed.reshape(det_local, total_time)


def splits_detectors(mesh, wigner, beam, offsets):
    count = mesh.shape["ord"]
    return (
        mesh.shape["det"] == 2
        and beam.shape[0] == 4 * count
        and wigner.shape[0] == 4 * CHUNKS * count
        and 2 * wigner.shape[0] == 4 * TILE
        and wigner.shape[1:3] == (2, TILE)
        and offsets.shape == (count, 32 * TILE)
        and count % BATCH == 0
        and count % PLANE == 0
    )


def solution(mesh):
    def run(wigner, alm, beam, crossing, offsets, fraction, taps):
        fused = splits_detectors(mesh, wigner, beam, offsets)
        return jax.shard_map(
            local_fused if fused else local,
            mesh=mesh,
            in_specs=(
                P("ord", None, None, "det"),
                P("ord", None),
                P(),
                P("ord"),
                P("ord"),
                P("ord"),
                P(),
            ),
            out_specs=P("det", "ord"),
            check_vma=False,
        )(wigner, alm, beam, crossing, offsets, fraction, taps)

    return run
```

```python
import functools
import math

import jax
import jax.numpy as jnp
import numpy as np
from jax import lax
from jax.experimental import pallas as pl
from jax.experimental.pallas import tpu as pltpu
from jax.sharding import PartitionSpec as P

TILE = 128
CHUNKS = 2
PLANE = 4
BATCH = 4
INFO_ROWS = 40
MESH = pl.DeviceIdType.MESH


def split_parts(values):
    high = values.astype(jnp.bfloat16)
    return high, (values - high.astype(jnp.float32)).astype(jnp.bfloat16)


def fourier_tables(orders_total, per):
    longitudes = 2 * orders_total
    order = np.arange(orders_total, dtype=np.int64)
    phase = (order[:, None] * np.arange(longitudes)[None, :]) % longitudes
    angle = phase * (2.0 * math.pi / longitudes)
    weight = np.where(order == 0, 1.0, 2.0)[:, None] / math.sqrt(longitudes)
    parts = np.stack([weight * np.cos(angle), -weight * np.sin(angle)], axis=1)
    parts = parts.reshape(orders_total, 2, longitudes // TILE, TILE)
    table = np.zeros((orders_total, per, 2, longitudes // TILE, per, TILE), np.float32)
    for det in range(per):
        table[:, det, :, :, det, :] = parts
    table = table.reshape(orders_total * per * 2, longitudes * per)
    high = table.astype(jnp.bfloat16)
    low = (table - high.astype(np.float32)).astype(jnp.bfloat16)
    return np.stack([high, low])


def kernel(
    count, per, intervals, tiles_per_item,
    wigner_hbm, beam_hbm, alm_hbm, table_hbm, crossing_ref, offsets_ref, fraction_ref, taps_ref,
    out_ref,
    beam_in, alm_in, beam_ref, alm_ref,
    wigner, table, partial_own, partial_out, partial_in, spectra_out, spectra_in,
    info_ref, info, picks, shifts, weights, band, field, cube, tiles, series,
    signal_out, signal_in, wide,
    small_sem, wigner_sem, table_sem, info_send, info_recv, column_send, column_recv, share_send, share_recv,
    pair_send, pair_recv, spec_send, spec_recv, out_send, out_recv,
):
    det = lax.axis_index("det")
    me = lax.axis_index("ord")
    partner = 1 - det
    orders = wigner.shape[0]
    chunk_orders = orders // CHUNKS
    blocks = shifts.shape[2]
    groups = tiles_per_item

    def wigner_copy(chunk):
        part = pl.ds(chunk * chunk_orders, chunk_orders)
        return pltpu.make_async_copy(wigner_hbm.at[part], wigner.at[part], wigner_sem.at[chunk])

    depth = beam_in.shape[2]
    near_depth = pl.ds(pl.multiple_of(det * depth, TILE), depth)
    beam_copy = pltpu.make_async_copy(beam_hbm.at[:, :, near_depth], beam_in, small_sem.at[0])
    alm_copy = pltpu.make_async_copy(alm_hbm.at[:, :, near_depth], alm_in, small_sem.at[1])
    beam_copy.start()
    alm_copy.start()
    for chunk in range(CHUNKS):
        wigner_copy(chunk).start()
    table_copy = pltpu.make_async_copy(table_hbm, table, table_sem)
    table_copy.start()

    barrier = pltpu.get_barrier_semaphore()

    def greet(step, carry):
        peer = lax.rem(me + step, count)
        pl.semaphore_signal(barrier, inc=1, device_id=(det, peer), device_id_type=MESH)
        return carry

    lax.fori_loop(1, count, greet, 0)
    pl.semaphore_signal(barrier, inc=1, device_id=(partner, me), device_id_type=MESH)

    def select_rows(source, wanted_column):
        chosen = jnp.where(
            wanted_column == lax.broadcasted_iota(jnp.int32, wanted_column.shape, 1), 1.0, 0.0
        ).astype(jnp.bfloat16)
        return jnp.dot(chosen, source, preferred_element_type=jnp.float32).astype(jnp.bfloat16)

    beams = wigner.shape[1]
    beam_copy.wait()
    beam_rows_all = beam_ref.shape[1]
    beam_source = beam_in[...].reshape(-1, depth)
    row = lax.broadcasted_iota(jnp.int32, (beam_rows_all, beam_source.shape[0]), 0)
    half_rows = beam_rows_all // 2
    side = lax.rem(row // half_rows + det, 2)
    beam_column = (side * (half_rows // 2) + row % half_rows // 2) * beams
    for beam_order in range(beams):
        beam_ref[beam_order] = select_rows(beam_source, beam_column + beam_order)
    alm_copy.wait()
    repeat = alm_ref.shape[1]
    alm_source = alm_in[...].reshape(-1, depth)
    row = lax.broadcasted_iota(jnp.int32, (orders * repeat, alm_source.shape[0]), 0)
    alm_ref[...] = select_rows(alm_source, row // repeat * 2 + row % 2).reshape(
        alm_ref.shape
    )

    half_blocks = blocks // 2
    near_blocks = pl.ds(pl.multiple_of(det * half_blocks, 8), half_blocks)
    info_ref[:half_blocks] = offsets_ref[near_blocks].astype(jnp.float32)
    info_ref[half_blocks : 2 * half_blocks] = fraction_ref[near_blocks]
    ids = jnp.broadcast_to(crossing_ref[...], (8, TILE))
    ids = ids % groups * (cube.shape[0] // groups) + ids // groups
    lanes_row = lax.broadcasted_iota(jnp.int32, (8, TILE), 1)
    info_ref[2 * half_blocks :] = jnp.take_along_axis(
        ids.astype(jnp.float32),
        lanes_row % blocks * groups + lanes_row // blocks,
        axis=1,
        mode="promise_in_bounds",
    )

    planes = count // PLANE
    near, plane = lax.rem(me, PLANE), me // PLANE

    def info_copy(step):
        return pltpu.make_async_remote_copy(
            src_ref=info_ref,
            dst_ref=info.at[det, near, plane],
            send_sem=info_send,
            recv_sem=info_recv,
            device_id=(det, lax.rem(me + step * PLANE, count)),
            device_id_type=MESH,
        )

    def column_copy(step):
        return pltpu.make_async_remote_copy(
            src_ref=info.at[det, near],
            dst_ref=info.at[det, near],
            send_sem=column_send,
            recv_sem=column_recv,
            device_id=(det, plane * PLANE + lax.rem(near + step, PLANE)),
            device_id_type=MESH,
        )

    def await_bytes(block, semaphore):
        pltpu.make_async_copy(block, block, semaphore).wait()

    rows = per * 2
    own_rows = count * rows

    def product(order, beam_order):
        alm_rows = alm_ref[order]
        beam_rows = beam_ref[beam_order]
        sky = beam_rows.reshape(-1, alm_rows.shape[0], depth) * alm_rows[None]
        return lax.dot_general(
            sky.reshape(-1, depth),
            wigner[order, beam_order],
            (((1,), (1,)), ((), ())),
            preferred_element_type=jnp.float32,
        )

    def multiply(chunk):
        wigner_copy(chunk).wait()

        def pair(step):
            first = chunk * chunk_orders + 2 * step
            place = pl.ds(step * 2 * rows, 2 * rows)
            for beam_order in range(wigner.shape[1]):
                lanes = pl.ds(beam_order * wigner.shape[2], wigner.shape[2])
                one = product(first, beam_order)
                two = product(first + 1, beam_order)
                for target, low in ((partial_own, 0), (partial_out, own_rows)):
                    target[chunk, :, place, lanes] = jnp.concatenate(
                        [
                            one[low : low + own_rows].reshape(count, rows, -1),
                            two[low : low + own_rows].reshape(count, rows, -1),
                        ],
                        axis=1,
                    )

        for step in range(chunk_orders // 2):
            pair(step)
            if step == chunk_orders // 4 - 1 and chunk > 0:
                spread(chunk - 1)

    def pair_copy(chunk):
        return pltpu.make_async_remote_copy(
            src_ref=partial_out.at[chunk],
            dst_ref=partial_in.at[chunk],
            send_sem=pair_send.at[chunk],
            recv_sem=pair_recv.at[chunk],
            device_id=(partner, me),
            device_id_type=MESH,
        )

    def spec_copy(chunk, target, source):
        return pltpu.make_async_remote_copy(
            src_ref=spectra_out.at[chunk, target],
            dst_ref=spectra_in.at[source, chunk],
            send_sem=spec_send.at[chunk],
            recv_sem=spec_recv.at[chunk],
            device_id=(det, target),
            device_id_type=MESH,
        )

    def spread(chunk):
        pair_copy(chunk).wait_recv()
        total = (partial_own[chunk] + partial_in[chunk]).astype(jnp.bfloat16)
        spectra_out[chunk] = total

        for step in range(count - 1):
            spec_copy(chunk, lax.rem(me + 1 + (step + PLANE - 1) % (count - 1), count), me).start()
        spectra_in[me, chunk] = spectra_out[chunk, me]

    for chunk in range(CHUNKS):
        multiply(chunk)
        if chunk == 0:
            pl.semaphore_wait(barrier, count)
            info[det, near, plane] = info_ref[...]
            for step in range(1, planes):
                info_copy(step).start()
        pair_copy(chunk).start()
        if chunk == CHUNKS // 2:
            await_bytes(info.at[det, near, pl.ds(0, planes - 1)], info_recv)
            for step in range(1, PLANE):
                column_copy(step).start()
    spread(CHUNKS - 1)

    await_bytes(info.at[det, pl.ds(0, PLANE - 1)], column_recv)
    share_copy = pltpu.make_async_remote_copy(
        src_ref=info.at[det],
        dst_ref=info.at[det],
        send_sem=share_send,
        recv_sem=share_recv,
        device_id=(partner, me),
        device_id_type=MESH,
    )
    share_copy.start()

    shape = (2 * TILE, TILE)
    place = lax.broadcasted_iota(jnp.int32, shape, 0)
    place = jnp.where(place < 3 * TILE // 2, place, place - 2 * TILE)
    lag = place - lax.broadcasted_iota(jnp.int32, shape, 1)
    reach = taps_ref.shape[0] // 2

    def add_tap(place, total):
        return jnp.where(lag == place - reach, taps_ref[place], total)

    band_values = lax.fori_loop(0, taps_ref.shape[0], add_tap, jnp.zeros(shape, jnp.float32))
    band_high, band_low = split_parts(band_values)
    band[:, :TILE] = band_high
    band[:, TILE:] = band_low

    pltpu.make_async_remote_copy(
        src_ref=info.at[partner],
        dst_ref=info.at[partner],
        send_sem=share_send,
        recv_sem=share_recv,
        device_id=(partner, me),
        device_id_type=MESH,
    ).wait_recv()

    lane = lax.broadcasted_iota(jnp.int32, (blocks, TILE), 1)
    each = TILE // groups
    group = lane // each
    items = cube.shape[0] // groups
    half_rows = blocks // 2

    places = lax.broadcasted_iota(jnp.int32, (TILE, TILE), 1).astype(jnp.float32)

    def prepare(n, carry):
        wanted = info[0, n % PLANE, n // PLANE, 2 * half_rows : 2 * half_rows + 1, :]
        ids = jnp.broadcast_to(wanted, (TILE, TILE)).T
        for part in range(cube.shape[0] // TILE):
            picks[n, :, part * TILE : (part + 1) * TILE] = jnp.where(
                ids - part * TILE == places, 1.0, 0.0
            ).astype(jnp.bfloat16)
        offset = jnp.concatenate([info[0, n % PLANE, n // PLANE, :half_rows], info[1, n % PLANE, n // PLANE, :half_rows]], axis=0)
        fraction = jnp.concatenate(
            [info[0, n % PLANE, n // PLANE, half_rows : 2 * half_rows], info[1, n % PLANE, n // PLANE, half_rows : 2 * half_rows]],
            axis=0,
        )
        for b in range(groups):
            spot = b * each + lane % each
            start = jnp.take_along_axis(offset, spot, axis=1, mode="promise_in_bounds")
            f = jnp.take_along_axis(fraction, spot, axis=1, mode="promise_in_bounds")
            shifts[n, b] = start.astype(jnp.int32) + group
            weights[n, b] = (
                jnp.where(group == 0, -1.0 / 6.0, f + 1.0)
                * jnp.where(group == 1, 0.5, f)
                * jnp.where(group == 2, -0.5, f - 1.0)
                * jnp.where(group == 3, 1.0 / 6.0, f - 2.0)
            )
        return carry

    lax.fori_loop(0, intervals, prepare, 0, unroll=2)

    table_copy.wait()
    chunk_rows = spectra_in.shape[2]
    for chunk in range(CHUNKS):
        await_bytes(spectra_in.at[pl.ds(0, count - 1), chunk], spec_recv.at[chunk])
        spectra = spectra_in[:, chunk].reshape(count * chunk_rows, items)
        turned = spectra.T
        for b in range(groups):
            columns = pl.ds(b * per * TILE, per * TILE)
            total = sum(
                jnp.dot(
                    turned, table[part, chunk, :, columns], preferred_element_type=jnp.float32
                )
                for part in range(2)
            )
            place = pl.ds(b * items, items)
            if chunk > 0:
                total = total + field[place]
            if chunk < CHUNKS - 1:
                field[place] = total
            else:
                cube[place] = total.astype(jnp.bfloat16)

    margin = 8
    for d in range(per):
        series[d, :margin] = jnp.zeros((margin, TILE), jnp.float32)
        series[d, margin + intervals * blocks :] = jnp.zeros((margin, TILE), jnp.float32)

    batch = tiles.shape[0] // TILE

    def sample(first, place_in_batch):
        n = first + place_in_batch
        near = pl.multiple_of(place_in_batch * TILE, TILE)
        for d in range(per):
            terms = [
                jnp.take_along_axis(
                    tiles[pl.ds(near + b * blocks, blocks), d * TILE : (d + 1) * TILE],
                    shifts[n, b],
                    axis=1,
                    mode="promise_in_bounds",
                )
                * weights[n, b]
                for b in range(groups)
            ]
            total = jnp.zeros((blocks, TILE), jnp.float32)
            for k in range(groups):
                moved = terms[(groups - 1 - k) % groups]
                for t in range(groups - 1):
                    moved = jnp.where(group == t, terms[(t - k) % groups], moved)
                if k:
                    moved = pltpu.roll(moved, TILE - k * each, 1)
                total = total + moved
            place = pl.ds(pl.multiple_of(margin + n * blocks, 8), blocks)
            series[d, place] = total.astype(jnp.bfloat16).astype(jnp.float32)

    def out_copy(target, source):
        return pltpu.make_async_remote_copy(
            src_ref=signal_out.at[target],
            dst_ref=signal_in.at[source],
            send_sem=out_send,
            recv_sem=out_recv,
            device_id=(det, target),
            device_id_type=MESH,
        )

    def smooth(targets):
        windows = []
        for n in targets:
            for d in range(per):
                rows_near = series[d, pl.ds(pl.multiple_of(n * blocks, 8), blocks + 2 * margin)]
                before, here, after = (
                    rows_near[margin + s : margin + s + blocks] for s in (-1, 0, 1)
                )
                sides = jnp.where(lane < TILE // 2, after, before)
                windows.append(jnp.concatenate([here, sides], axis=1))
        window = jnp.concatenate(windows, axis=0).astype(jnp.bfloat16)
        both = jnp.dot(window, band[...], preferred_element_type=jnp.float32)
        smoothed = (both[:, :TILE] + both[:, TILE:]).astype(jnp.bfloat16)
        smoothed = smoothed.reshape(len(targets), per, blocks, TILE)
        for place, n in enumerate(targets):
            signal_out[n] = smoothed[place]

    def send(target):
        @pl.when(target != me)
        def _():
            out_copy(target, me).start()

    batches = intervals // batch
    origin = (me // batch + 1) * batch

    def one_batch(turn, carry):
        first = lax.rem(origin + turn * batch, intervals)
        chosen = picks[pl.ds(first, batch)].reshape(batch * TILE, -1)
        tiles[...] = jnp.dot(chosen, cube[...], preferred_element_type=jnp.float32)
        for step in range(batch):
            sample(first, step)
        targets = [lax.rem(first + intervals - 1 + step, intervals) for step in range(batch)]

        @pl.when(turn == 0)
        def _():
            smooth(targets[2:])

        @pl.when(turn > 0)
        def _():
            smooth(targets)
            for target in targets[:2]:
                send(target)

        for target in targets[2:]:
            send(target)
        return carry

    lax.fori_loop(0, batches, one_batch, 0)
    targets = [lax.rem(origin + intervals - 1 + step, intervals) for step in range(2)]
    smooth(targets)
    for target in targets:
        send(target)

    signal_in[me] = signal_out[me]
    await_bytes(signal_in.at[pl.ds(0, count - 1)], out_recv)
    wide[...] = signal_in[...].astype(jnp.float32).reshape(wide.shape)
    rows_out = out_ref.shape[0]
    for block in range(blocks):
        parts = [
            wide[pl.ds(first * blocks + block, 8, stride=blocks), :]
            for first in range(0, rows_out, 8)
        ]
        out_ref[:, block * TILE : (block + 1) * TILE] = jnp.concatenate(parts, axis=0).astype(
            out_ref.dtype
        )

    await_bytes(info.at[det, near, pl.ds(0, planes - 1)], info_send)
    await_bytes(info.at[det, pl.ds(0, PLANE - 1)], column_send)
    await_bytes(signal_out.at[pl.ds(0, count - 1)], out_send)
    for chunk in range(CHUNKS):
        await_bytes(spectra_out.at[chunk, pl.ds(0, count - 1)], spec_send.at[chunk])
    for chunk in range(CHUNKS):
        pair_copy(chunk).wait_send()
    share_copy.wait_send()


def local_fused(wigner, alm, beam, crossing, offsets, fraction, taps):
    det_count = lax.axis_size("det")
    count = lax.axis_size("ord")
    orders, beams, lats, depth = wigner.shape
    dets = beam.shape[0]
    per = dets // det_count // count
    orders_total = orders * count
    longitudes = 2 * orders_total
    groups = longitudes // TILE
    items = beams * lats
    tiles = items * groups
    intervals = count
    blocks = offsets.shape[1] // TILE
    chunk_rows = orders // CHUNKS * per * 2

    table = fourier_tables(orders_total, per).reshape(
        2, count, CHUNKS, chunk_rows, longitudes * per
    )
    table = jnp.asarray(
        np.swapaxes(table, 1, 2).reshape(2, CHUNKS, count * chunk_rows, longitudes * per)
    )

    f32, bf16 = jnp.float32, jnp.bfloat16
    dma = pltpu.SemaphoreType.DMA
    vmem = pl.BlockSpec(memory_space=pltpu.VMEM)
    anywhere = pl.BlockSpec(memory_space=pl.ANY)
    partial = pltpu.VMEM((CHUNKS, count, chunk_rows, items), f32)
    outgoing = pltpu.VMEM((CHUNKS, count, chunk_rows, items), bf16)
    arriving = pltpu.VMEM((count, CHUNKS, chunk_rows, items), bf16)
    result = pl.pallas_call(
        functools.partial(kernel, count, per, intervals, groups),
        out_shape=jax.ShapeDtypeStruct((count * per, blocks * TILE), bf16),
        in_specs=[
            anywhere, anywhere, anywhere, anywhere, vmem, vmem, vmem,
            pl.BlockSpec(memory_space=pltpu.SMEM),
        ],
        out_specs=vmem,
        scratch_shapes=[
            pltpu.VMEM((dets, beams, depth), bf16),
            pltpu.VMEM((orders, 2, depth), bf16),
            pltpu.VMEM((beams, dets * 2, depth), bf16),
            pltpu.VMEM((orders, 16, depth), bf16),
            pltpu.VMEM(wigner.shape, bf16),
            pltpu.VMEM(table.shape, bf16),
            partial, partial, partial, outgoing, arriving,
            pltpu.VMEM((INFO_ROWS, TILE), f32),
            pltpu.VMEM((2, PLANE, count // PLANE, INFO_ROWS, TILE), f32),
            pltpu.VMEM((intervals, TILE, tiles), bf16),
            pltpu.VMEM((intervals, groups, blocks, TILE), jnp.int32),
            pltpu.VMEM((intervals, groups, blocks, TILE), f32),
            pltpu.VMEM((2 * TILE, 2 * TILE), bf16),
            pltpu.VMEM((tiles, per * TILE), f32),
            pltpu.VMEM((tiles, per * TILE), bf16),
            pltpu.VMEM((BATCH * TILE, per * TILE), f32),
            pltpu.VMEM((per, intervals * blocks + 16, TILE), f32),
            pltpu.VMEM((count, per, blocks, TILE), bf16),
            pltpu.VMEM((count, per, blocks, TILE), bf16),
            pltpu.VMEM((count * per * blocks, TILE), f32),
            dma((2,)), dma((CHUNKS,)), dma, dma, dma, dma, dma, dma, dma,
            dma((CHUNKS,)), dma((CHUNKS,)), dma((CHUNKS,)), dma((CHUNKS,)),
            dma, dma,
        ],
        compiler_params=pltpu.CompilerParams(
            collective_id=0, has_side_effects=True, vmem_limit_bytes=56 * 2**20
        ),
    )(
        wigner,
        beam,
        alm,
        table,
        crossing,
        offsets.reshape(blocks, TILE),
        fraction.reshape(blocks, TILE),
        taps,
    )
    return result.astype(f32)


def with_halo(cells, sides, width):
    for axis, dim in sides:
        count = lax.axis_size(axis)
        ends = count - 1
        head = lax.slice_in_dim(cells, 0, width, axis=dim)
        tail = lax.slice_in_dim(cells, cells.shape[dim] - width, cells.shape[dim], axis=dim)
        cells = jnp.concatenate(
            [
                lax.ppermute(tail, axis, [(i, (i + 1) % count) for i in range(ends)]),
                cells,
                lax.ppermute(head, axis, [((i + 1) % count, i) for i in range(ends)]),
            ],
            axis=dim,
        )
    return cells


def lagrange_weights(position):
    shifted = position + 1.0
    minus_one = position - 1.0
    minus_two = position - 2.0
    return (
        -position * minus_one * minus_two / 6.0,
        shifted * minus_one * minus_two / 2.0,
        -shifted * position * minus_two / 2.0,
        shifted * position * minus_one / 6.0,
    )


def stencil_matrix(offset_part, fraction_part, width):
    columns = jnp.arange(width, dtype=jnp.int32)
    distance = columns[:, None] - offset_part[..., None, :]
    factors = lagrange_weights(fraction_part[..., None, :])
    matrix = jnp.zeros(distance.shape, jnp.float32)
    for place in range(4):
        matrix = matrix + jnp.where(distance == place, factors[place], 0.0)
    return matrix


def sky_beam(alm_part, beam_part):
    product = (
        beam_part.astype(jnp.float32)[:, None, :, None, :]
        * alm_part.astype(jnp.float32)[None, :, None, :, :]
    )
    return product.astype(jnp.bfloat16)


def local(wigner, alm, beam, crossing, offsets, fraction, taps):
    det_count = lax.axis_size("det")
    det_index = lax.axis_index("det")
    ord_count = lax.axis_size("ord")
    orders_local = wigner.shape[0]
    half_width = wigner.shape[3]
    det_local = beam.shape[0] // det_count
    alm_half = lax.dynamic_slice_in_dim(alm, det_index * half_width, half_width, 2)
    beam_half = lax.dynamic_slice_in_dim(beam, det_index * half_width, half_width, 2)
    spectra = lax.psum_scatter(
        jnp.einsum(
            "mkrl,jmkcl->jkrcm",
            wigner,
            sky_beam(alm_half, beam_half),
            preferred_element_type=jnp.float32,
        ),
        "det",
        scatter_dimension=0,
        tiled=True,
    )
    items_all = wigner.shape[1] * wigner.shape[2]
    outgoing = spectra.astype(jnp.bfloat16).reshape(det_local, items_all, 2 * orders_local)
    arrived = lax.all_to_all(outgoing, "ord", split_axis=1, concat_axis=2, tiled=True)
    items_local = items_all // ord_count
    spectrum = arrived.reshape(det_local, items_local, ord_count, 2, orders_local).astype(
        jnp.float32
    )
    orders_total = ord_count * orders_local
    longitudes = 2 * orders_total
    block = math.gcd(512, longitudes)
    order_ids = (
        jnp.arange(ord_count, dtype=jnp.int32)[:, None] * orders_local
        + jnp.arange(orders_local, dtype=jnp.int32)[None, :]
    )
    weight_row = (jnp.where(order_ids == 0, 1.0, 2.0) / math.sqrt(longitudes))[:, :, None]
    step_angle = 2.0 * math.pi / longitudes
    base_phase = (
        order_ids[:, :, None] * jnp.arange(block, dtype=jnp.int32)[None, None, :] % longitudes
    )
    base_angle = base_phase.astype(jnp.float32) * step_angle
    base_cos = jnp.cos(base_angle)
    base_sin = jnp.sin(base_angle)
    pieces = []
    for first in range(0, longitudes, block):
        shift_angle = (order_ids * first % longitudes).astype(jnp.float32)[:, :, None] * step_angle
        shift_cos = jnp.cos(shift_angle)
        shift_sin = jnp.sin(shift_angle)
        cos_block = base_cos * shift_cos - base_sin * shift_sin
        sin_block = base_sin * shift_cos + base_cos * shift_sin
        table = jnp.stack([weight_row * cos_block, -weight_row * sin_block], axis=1)
        pieces.append(
            jnp.einsum("jincs,ncsp->ijp", spectrum, table, precision=lax.Precision.HIGHEST)
        )
    cube = jnp.concatenate(pieces, axis=2).astype(jnp.bfloat16)
    tile_width = TILE
    blocks_per_item = longitudes // tile_width
    tiles = cube.reshape(items_local, det_local, blocks_per_item, tile_width).transpose(0, 2, 1, 3)
    tiles = tiles.reshape(items_local * blocks_per_item, det_local, tile_width)
    tiles_local = tiles.shape[0]
    wanted = crossing[0]
    crossings = wanted.shape[0]
    capacity = max(2, 2 * crossings // ord_count)
    holder = wanted // tiles_local
    local_ids = wanted % tiles_local
    order_index = jnp.arange(crossings, dtype=jnp.int32)
    earlier = (holder[:, None] == holder[None, :]) & (order_index[None, :] < order_index[:, None])
    slot_ids = jnp.sum(earlier.astype(jnp.int32), axis=1)
    flat_slot = holder * capacity + slot_ids
    chosen = flat_slot[:, None] == jnp.arange(ord_count * capacity, dtype=jnp.int32)[None, :]
    requests = (jnp.sum(jnp.where(chosen, local_ids[:, None] + 1, 0), axis=0) - 1).reshape(
        ord_count, capacity
    )
    offset_rows = offsets[0].reshape(crossings, -1)
    fraction_rows = fraction[0].reshape(crossings, -1)
    samples_each = offset_rows.shape[1]
    slot_crossing = jnp.sum(jnp.where(chosen, order_index[:, None], 0), axis=0)
    occupied = jnp.any(chosen, axis=0)
    slot_offsets = jnp.where(occupied[:, None], offset_rows[slot_crossing], 0)
    slot_offsets = slot_offsets.reshape(ord_count, capacity, samples_each)
    slot_fractions = jnp.where(occupied[:, None], fraction_rows[slot_crossing], 0.0)
    slot_fractions = slot_fractions.reshape(ord_count, capacity, samples_each)
    asked = lax.all_to_all(requests, "ord", split_axis=0, concat_axis=0, tiled=True)
    asked_offsets = lax.all_to_all(slot_offsets, "ord", split_axis=0, concat_axis=0, tiled=True)
    asked_fractions = lax.all_to_all(slot_fractions, "ord", split_axis=0, concat_axis=0, tiled=True)
    stencil = stencil_matrix(asked_offsets, asked_fractions, tile_width)
    present = asked >= 0
    picked = tiles[jnp.maximum(asked, 0)]
    result = jnp.einsum(
        "rnjo,rnos->rnjs",
        jnp.where(present[..., None, None], picked, jnp.zeros((), jnp.bfloat16)).astype(
            jnp.float32
        ),
        stencil,
        precision=lax.Precision.HIGHEST,
    )
    received = lax.all_to_all(
        result.astype(jnp.bfloat16), "ord", split_axis=0, concat_axis=0, tiled=True
    )
    samples = jnp.transpose(received[holder, slot_ids], (1, 0, 2)).reshape(det_local, -1)
    reach = taps.shape[0] // 2
    extended = with_halo(samples, (("ord", 1),), reach)
    total_time = samples.shape[1]
    padded = jnp.concatenate(
        [extended, jnp.zeros((det_local, 128 - 2 * reach), jnp.bfloat16)], axis=1
    )
    windows = jnp.concatenate(
        [
            padded[:, :total_time].reshape(det_local, -1, 128),
            padded[:, 128 : total_time + 128].reshape(det_local, -1, 128),
        ],
        axis=2,
    )
    lag_index = (
        jnp.arange(256, dtype=jnp.int32)[:, None] - jnp.arange(128, dtype=jnp.int32)[None, :]
    )
    inside = (lag_index >= 0) & (lag_index < taps.shape[0])
    banded = jnp.where(inside, taps[jnp.clip(lag_index, 0, taps.shape[0] - 1)], 0.0)
    smoothed = jnp.einsum(
        "jbu,uo->jbo", windows.astype(jnp.float32), banded, precision=lax.Precision.HIGHEST
    )
    return smoothed.reshape(det_local, total_time)


def splits_detectors(mesh, wigner, beam, offsets):
    count = mesh.shape["ord"]
    return (
        mesh.shape["det"] == 2
        and beam.shape[0] == 4 * count
        and wigner.shape[0] == 16 * count
        and 2 * wigner.shape[0] == 4 * TILE
        and wigner.shape[1:3] == (2, TILE)
        and offsets.shape == (count, 32 * TILE)
        and count % BATCH == 0
        and count % PLANE == 0
    )


def solution(mesh):
    def run(wigner, alm, beam, crossing, offsets, fraction, taps):
        fused = splits_detectors(mesh, wigner, beam, offsets)
        return jax.shard_map(
            local_fused if fused else local,
            mesh=mesh,
            in_specs=(
                P("ord", None, None, "det"),
                P("ord", None),
                P(),
                P("ord"),
                P("ord"),
                P("ord"),
                P(),
            ),
            out_specs=P("det", "ord"),
            check_vma=False,
        )(wigner, alm, beam, crossing, offsets, fraction, taps)

    return run
```
